256 devices in a mesh: rows: 64 (over y, z, core), cols: 4 (over x).
Axes of the slice: x: 4, y: 4, z: 8, core: 2. Of those that a mesh axis runs over, the one named last changes fastest.
Arguments:
- user_factors: float32 [128, 131072], P('cols', 'rows'), may hold values from -6 to 6
- item_factors: bfloat16 [128, 524288], P('cols', 'rows'), may hold values from -0.0078125 to 0.0078125
- tile_user: int32 [4608], P('rows'), may hold values from 0 to 7
- tile_item: int32 [4608], P('rows'), may hold values from 0 to 2047, as said below
- tile_count: int32 [64], P('rows'), may hold values from 36 to 72, as said below
- tile_mask: bfloat16 [4608, 256, 256], P('rows'), may hold values from 0 to 2, as said below
Outputs:
- solution_field: float32 [128, 131072], P('cols', 'rows')
- residual: float32 [128, 131072], P('cols', 'rows')
The draws below stay inside these ranges and needn't reach their ends.
Inputs may be any that keep to these rules, and one draw needn't show every extreme that they name: `tile_item`: item block b is held by index b // 32 of rows. Among the live slots of one index of rows at most 2 name item blocks held by one index of rows, and in every draw some index reaches 2. `tile_count`: some index of rows has all 72 slots live in every draw. `tile_mask`: each entry is zero or a strength of 0.5 or more.
All inputs are finite; a program needn't handle non-finite values.
Results may differ from the reference program's by a relative error of at most 0.0008.
Values may be sent and summed in bfloat16 or wider, within the bound.
A program may use at most 128 MiB of HBM per device.

```python
import jax
import jax.numpy as jnp
from jax import lax

K = 128
TILE = 256
ITERS = 2
UBLK_DEV = 8
IBLK_DEV = 32
TILES_DEV = 72
CAP = 2
USERS = 131072
ITEMS = 524288
N_ROWS = 64


def draw_tile_item(key, part):
    key = jax.random.fold_in(key, 11)

    def one_device(device):
        device_key = jax.random.fold_in(key, device)
        first_key, second_key = jax.random.split(device_key)
        owners = jax.random.permutation(first_key, N_ROWS).astype(jnp.int32)
        order = jnp.arange(TILES_DEV, dtype=jnp.int32)
        holder = owners[order // CAP % N_ROWS]
        blocks = jax.random.randint(second_key, (TILES_DEV,), 0, IBLK_DEV, dtype=jnp.int32)
        return holder * IBLK_DEV + blocks
    return jax.vmap(one_device)(jnp.arange(N_ROWS, dtype=jnp.int32)).reshape(N_ROWS * TILES_DEV).astype(jnp.int32)


def draw_tile_count(key, part):
    key = jax.random.fold_in(key, 23)
    first_key, second_key = jax.random.split(key)
    counts = jax.random.randint(first_key, (N_ROWS,), max(1, TILES_DEV // 2), TILES_DEV + 1, dtype=jnp.int32)
    fullest = jax.random.randint(second_key, (), 0, N_ROWS, dtype=jnp.int32)
    places = jnp.arange(N_ROWS, dtype=jnp.int32)
    return jnp.where(places == fullest, TILES_DEV, counts).astype(jnp.int32)


def draw_tile_mask(key, part):
    key = jax.random.fold_in(key, 37)
    first_key, second_key = jax.random.split(key)
    shape = (N_ROWS * TILES_DEV, TILE, TILE)
    present = (jax.random.uniform(first_key, shape, dtype=jnp.float32) < 0.5).astype(jnp.float32)
    spread = jax.random.uniform(second_key, shape, dtype=jnp.float32)
    strength = 0.5 * jnp.exp(spread * jnp.log(4.0))
    return (present * strength).astype(jnp.bfloat16)


def set_ends(entries, own_key, low, largest):
    longest = entries.shape.index(max(entries.shape))
    spots = []
    for shift in (0, 1):
        where = [jax.random.randint(jax.random.fold_in(own_key, axis), (), 0, length) for axis, length in enumerate(entries.shape)]
        where[longest] = (where[longest] + shift) % entries.shape[longest]
        spots.append(tuple(where))
    return entries.at[spots[0]].set(low).at[spots[1]].set(largest)


def steps_of(own_key, shape, cuts, least, largest):
    gain = 1.0
    for dim, shards_of in cuts:
        heights = jax.random.uniform(jax.random.fold_in(jax.random.fold_in(own_key, 6), dim), (shards_of,), jnp.float32, least / len(cuts), largest / len(cuts))
        gain = gain * jnp.repeat(jnp.exp(heights), shape[dim] // shards_of).reshape((-1,) + (1,) * (len(shape) - 1 - dim))
    return gain


def gaussian(stream_key, dims, scale, reach, cuts=(), held_as=jnp.bfloat16):
    level = steps_of(stream_key, dims, cuts, -0.22, 0.18) if cuts else 1.0
    entries = jax.random.normal(stream_key, dims, jnp.float32) * scale * level
    return jnp.minimum(jnp.maximum(entries, -reach), reach).astype(held_as)


def setup_inputs(seed: int = 0) -> dict:
    key_list = jax.random.split(jax.random.key(seed), 7)
    return {
        "user_factors": gaussian(key_list[0], (K, USERS), 1.0, 6.0, ((0, 4), (1, 64)), jnp.float32),
        "item_factors": gaussian(key_list[1], (K, ITEMS), ITEMS ** -0.5, 0.0078125, ((0, 4), (1, 64))),
        "tile_user": set_ends(jax.random.randint(key_list[2], (N_ROWS * TILES_DEV,), 0, UBLK_DEV), jax.random.fold_in(key_list[2], 1), 0, UBLK_DEV - 1).astype(jnp.int32),
        "tile_item": draw_tile_item(jax.random.fold_in(key_list[6], 71), 0),
        "tile_count": draw_tile_count(jax.random.fold_in(key_list[6], 71), 0),
        "tile_mask": draw_tile_mask(jax.random.fold_in(key_list[6], 71), 0),
    }


ridge = 0.5
confidence = 40.0
highest = lax.Precision.HIGHEST


def collect_blocks(users_dev, terms):
    select = (users_dev[None, :] == jnp.arange(UBLK_DEV, dtype=jnp.int32)[:, None]).astype(jnp.float32)
    summed = jnp.einsum('bt,tuc->buc', select, terms, precision=highest)
    return summed.reshape(UBLK_DEV * TILE, terms.shape[2])


def device_terms(item_table, items_dev, strengths_dev, live_dev):
    item_tiles = item_table.reshape(-1, TILE, K)[items_dev]
    masks = strengths_dev.astype(jnp.float32) * live_dev[:, None, None]
    return item_tiles, masks


def reference(user_factors, item_factors, tile_user, tile_item, tile_count, tile_mask):
    item_table = item_factors.astype(jnp.float32).T
    gram = jnp.dot(item_table.T, item_table, precision=highest)
    users_all = tile_user.reshape(N_ROWS, TILES_DEV)
    items_all = tile_item.reshape(N_ROWS, TILES_DEV)
    strengths_all = tile_mask.reshape(N_ROWS, TILES_DEV, TILE, TILE)
    order = jnp.arange(TILES_DEV, dtype=jnp.int32)
    live_all = (order[None, :] < tile_count[:, None]).astype(jnp.float32)

    def rhs_dev(pack):
        users_dev, items_dev, strengths_dev, live_dev = pack
        item_tiles, masks = device_terms(item_table, items_dev, strengths_dev, live_dev)
        terms = jnp.einsum('tui,tic->tuc', masks, item_tiles, precision=highest)
        return collect_blocks(users_dev, terms)

    right_side = (1.0 + confidence) * lax.map(rhs_dev, (users_all, items_all, strengths_all, live_all)).reshape(USERS, K)

    def apply_op(dirs):
        dev_dirs = dirs.reshape(N_ROWS, UBLK_DEV * TILE, K)

        def one_dev(pack):
            dirs_dev, users_dev, items_dev, strengths_dev, live_dev = pack
            item_tiles, masks = device_terms(item_table, items_dev, strengths_dev, live_dev)
            dir_tiles = dirs_dev.reshape(UBLK_DEV, TILE, K)[users_dev]
            scores = jnp.einsum('tuk,tik->tui', dir_tiles, item_tiles, precision=highest) * masks
            terms = jnp.einsum('tui,tic->tuc', scores, item_tiles, precision=highest)
            return collect_blocks(users_dev, terms)

        sparse = lax.map(one_dev, (dev_dirs, users_all, items_all, strengths_all, live_all)).reshape(USERS, K)
        return jnp.dot(dirs, gram, precision=highest) + ridge * dirs + confidence * sparse

    solution_field = user_factors.T
    residual = right_side - apply_op(solution_field)
    direction = residual
    norm_now = jnp.sum(residual * residual)
    for iteration in range(ITERS):
        image = apply_op(direction)
        alpha = norm_now / jnp.sum(direction * image)
        solution_field = solution_field + alpha * direction
        residual = residual - alpha * image
        norm_next = jnp.sum(residual * residual)
        direction = residual + (norm_next / norm_now) * direction
        norm_now = norm_next
    return solution_field.T, residual.T
```

```python
import jax
import jax.numpy as jnp
from jax import lax
from jax.experimental import pallas as pl
from jax.experimental.pallas import tpu as pltpu
from jax.sharding import PartitionSpec as P

RIDGE = 0.5
CONFIDENCE = 40.0
HIGHEST = lax.Precision.HIGHEST
MESH = pl.DeviceIdType.MESH
F32 = jnp.float32
BF16 = jnp.bfloat16
Y_CHIPS = 4
GROUP = 16
VMEM_BYTES = 48 * 1024 * 1024


def half_lanes(shape):
    return lax.broadcasted_iota(jnp.int32, shape, 1) < 64


def cg_kernel(
    perm_ref, user_ref, keep_ref, live_ref, last_ref, has_ref,
    users_ref, items_ref, tiles_ref, mask_ref,
    solution_ref, residual_ref,
    masks, users_send, users_recv, items_recv, gram_part, gram_recv, gram_piece, gram_all, gram,
    sums_send, sums_recv, halves, terms, state_x, state_r, state_q, image, out_send, out_recv,
    mask_sem, x_send_sems, x_recv_sems, i_send_sems, i_recv_sems, g_send_sems, g_recv_sems,
    s_send_sems, s_recv_sems, o_send_sems, o_recv_sems,
):
    row = lax.axis_index("rows")
    col = lax.axis_index("cols")
    n_cols = lax.axis_size("cols")
    own_a = lax.rem(row, GROUP)
    own_y = lax.div(row, GROUP)
    own_b = col * Y_CHIPS + own_y
    tile_total, own_users, tile_cols = masks.shape
    col_width = users_ref.shape[0]
    blocks = halves.shape[0]
    item_quarter = items_recv.shape[1]

    def peer_a(j):
        return (own_y * GROUP + j, col)

    def peer_b(j):
        return (lax.rem(j, Y_CHIPS) * GROUP + own_a, lax.div(j, Y_CHIPS))

    def others(own, count, body):
        def step(i, carry):
            body(lax.rem(own + i, count))
            return carry

        lax.fori_loop(1, count, step, 0)

    mask_copy = pltpu.make_async_copy(
        mask_ref.at[:, pl.ds(pl.multiple_of(col * own_users, own_users), own_users), :], masks, mask_sem
    )
    mask_copy.start()

    barrier = pltpu.get_barrier_semaphore()
    others(own_a, GROUP, lambda j: pl.semaphore_signal(barrier, inc=1, device_id=peer_a(j), device_id_type=MESH))
    others(own_b, GROUP, lambda j: pl.semaphore_signal(barrier, inc=1, device_id=peer_b(j), device_id_type=MESH))

    for dest in range(n_cols):
        for pair in range(blocks // 2):
            first = users_ref[:, pl.ds((2 * pair) * 256 + (dest // 2) * 128, 128)]
            second = users_ref[:, pl.ds((2 * pair + 1) * 256 + (dest // 2) * 128, 128)]
            low = half_lanes(first.shape)
            if dest % 2 == 0:
                joined = jnp.where(low, first, pltpu.roll(second, 64, 1))
            else:
                joined = jnp.where(low, pltpu.roll(first, 64, 1), second)
            users_send[dest, :, pl.ds(pair * 128, 128)] = joined
    pl.semaphore_wait(barrier, 2 * (GROUP - 1))

    def item_copy(j):
        return pltpu.make_async_remote_copy(
            src_ref=items_ref.at[:, pl.ds(pl.multiple_of(j * item_quarter, item_quarter), item_quarter)],
            dst_ref=items_recv.at[pl.ds(pl.multiple_of(col * col_width, col_width), col_width)],
            send_sem=i_send_sems.at[j], recv_sem=i_recv_sems.at[col],
            device_id=(row, j), device_id_type=MESH,
        )

    def item_arrival(j):
        return pltpu.make_async_remote_copy(
            src_ref=items_ref.at[:, pl.ds(pl.multiple_of(j * item_quarter, item_quarter), item_quarter)],
            dst_ref=items_recv.at[pl.ds(pl.multiple_of(j * col_width, col_width), col_width)],
            send_sem=i_send_sems.at[j], recv_sem=i_recv_sems.at[j],
            device_id=(row, j), device_id_type=MESH,
        )

    def user_copy(j):
        return pltpu.make_async_remote_copy(
            src_ref=users_send.at[j], dst_ref=users_recv.at[pl.ds(pl.multiple_of(col * col_width, col_width), col_width)],
            send_sem=x_send_sems.at[j], recv_sem=x_recv_sems.at[col],
            device_id=(row, j), device_id_type=MESH,
        )

    def user_arrival(j):
        return pltpu.make_async_remote_copy(
            src_ref=users_send.at[j], dst_ref=users_recv.at[pl.ds(pl.multiple_of(j * col_width, col_width), col_width)],
            send_sem=x_send_sems.at[j], recv_sem=x_recv_sems.at[j],
            device_id=(row, j), device_id_type=MESH,
        )

    others(col, n_cols, lambda j: item_copy(j).start())
    others(col, n_cols, lambda j: user_copy(j).start())
    own_rows = pl.ds(pl.multiple_of(col * col_width, col_width), col_width)
    items_recv[own_rows, :] = items_ref[:, pl.ds(pl.multiple_of(col * item_quarter, item_quarter), item_quarter)]
    users_recv[own_rows, :] = users_send[col]

    others(col, n_cols, lambda j: item_arrival(j).wait_recv())
    table = items_recv[...]
    gram_part[...] = lax.dot_general(
        table, table, (((1,), (1,)), ((), ())), preferred_element_type=F32
    ).reshape(gram_part.shape)

    def gram_copy(stage, src, dst, slot, j, peer):
        return pltpu.make_async_remote_copy(
            src_ref=src, dst_ref=dst, send_sem=g_send_sems.at[stage, j], recv_sem=g_recv_sems.at[stage, slot],
            device_id=peer(j), device_id_type=MESH,
        )

    def gram_first(j, slot):
        return gram_copy(0, gram_part.at[j], gram_recv.at[slot], slot, j, peer_a)

    def gram_second(j, slot):
        return gram_copy(1, gram_piece, gram_all.at[slot], slot, j, peer_b)

    def gram_third(j, slot):
        return gram_copy(2, gram.at[own_a], gram.at[slot], slot, j, peer_a)

    others(own_a, GROUP, lambda j: gram_first(j, own_a).start())
    gram_recv[own_a] = gram_part[own_a]
    others(own_a, GROUP, lambda j: gram_first(j, j).wait_recv())
    gram_piece[...] = jnp.sum(gram_recv[...], axis=0)
    others(own_b, GROUP, lambda j: gram_second(j, own_b).start())
    gram_all[own_b] = gram_piece[...]
    others(own_b, GROUP, lambda j: gram_second(j, j).wait_recv())
    gram[own_a] = jnp.sum(gram_all[...], axis=0)
    others(own_a, GROUP, lambda j: gram_third(j, own_a).start())

    others(col, n_cols, lambda j: user_arrival(j).wait_recv())
    state_x[...] = users_recv[...].T
    mask_copy.wait()

    def sparse_part(vectors, first_time):
        high = vectors.astype(BF16)
        low = (vectors - high.astype(F32)).astype(BF16)
        halves[:, :, :128] = high.reshape(blocks, own_users, 128)
        halves[:, :, 128:] = low.reshape(blocks, own_users, 128)

        def step(s, running):
            item = tiles_ref[s]
            scores = jnp.dot(
                halves[user_ref[s]], jnp.concatenate([item, item], axis=0), preferred_element_type=F32
            )
            mask = masks[perm_ref[s]].astype(F32) * live_ref[s]
            if first_time:
                strengths = mask * ((1.0 + CONFIDENCE) - CONFIDENCE * scores)
            else:
                strengths = mask * scores
            s_high = strengths.astype(BF16)
            s_low = (strengths - s_high.astype(F32)).astype(BF16)
            both = lax.dot_general(
                jnp.concatenate([s_high, s_low], axis=0), item, (((1,), (1,)), ((), ())),
                preferred_element_type=F32,
            )
            running = both[:own_users] + both[own_users:] + keep_ref[s] * running
            terms[s] = running
            return running

        lax.fori_loop(0, tile_total, step, jnp.zeros((own_users, 128), F32), unroll=4)
        return jnp.concatenate([terms[last_ref[b]] * has_ref[b] for b in range(blocks)], axis=0)

    def dense_part(vectors):
        return (
            jnp.dot(vectors, gram[...].reshape(128, 128), precision=HIGHEST, preferred_element_type=F32)
            + RIDGE * vectors
        )

    def all_sums(round_index, products):
        rows = [jnp.sum(p, axis=0, keepdims=True) for p in products]
        rows.append(jnp.zeros((8 - len(rows), 128), F32))
        total = jnp.concatenate(rows, axis=0)
        for stage, (peer, own) in enumerate(((peer_a, own_a), (peer_b, own_b))):
            at = 2 * round_index + stage

            def copy(j, slot, at=at, peer=peer):
                return pltpu.make_async_remote_copy(
                    src_ref=sums_send.at[at], dst_ref=sums_recv.at[at, slot],
                    send_sem=s_send_sems.at[at, j], recv_sem=s_recv_sems.at[at, slot],
                    device_id=peer(j), device_id_type=MESH,
                )

            sums_send[at] = total
            others(own, GROUP, lambda j: copy(j, own).start())
            sums_recv[at, own] = total
            others(own, GROUP, lambda j: copy(j, j).wait_recv())
            total = jnp.sum(sums_recv[at], axis=0)
            others(own, GROUP, lambda j: copy(j, j).wait_send())
        total = jnp.sum(total, axis=1, keepdims=True)
        return [total[i : i + 1, :] for i in range(len(products))]

    start = sparse_part(state_x[...], True)
    others(own_a, GROUP, lambda j: gram_third(j, j).wait_recv())
    state_r[...] = start - dense_part(state_x[...])

    image[...] = dense_part(state_r[...]) + CONFIDENCE * sparse_part(state_r[...], False)
    norm_0, curve_0 = all_sums(0, [state_r[...] * state_r[...], state_r[...] * image[...]])
    alpha_0 = norm_0 / curve_0
    state_q[...] = state_r[...]
    state_x[...] = state_x[...] + alpha_0 * state_r[...]
    state_r[...] = state_r[...] - alpha_0 * image[...]

    image_r = dense_part(state_r[...]) + CONFIDENCE * sparse_part(state_r[...], False)
    norm_1, curve_rr, curve_rd, curve_dr = all_sums(
        1,
        [
            state_r[...] * state_r[...],
            state_r[...] * image_r,
            state_r[...] * image[...],
            state_q[...] * image_r,
        ],
    )
    beta = norm_1 / norm_0
    alpha_1 = norm_1 / (curve_rr + beta * (curve_rd + curve_dr) + beta * beta * curve_0)
    out_x = state_x[...] + alpha_1 * (state_r[...] + beta * state_q[...])
    out_r = state_r[...] - alpha_1 * (image_r + beta * image[...])

    out_send[0] = out_x.T.reshape(n_cols, col_width, blocks * own_users)
    out_send[1] = out_r.T.reshape(n_cols, col_width, blocks * own_users)

    def out_copy(j, slot):
        return pltpu.make_async_remote_copy(
            src_ref=out_send.at[:, j], dst_ref=out_recv.at[slot],
            send_sem=o_send_sems.at[j], recv_sem=o_recv_sems.at[slot],
            device_id=(row, j), device_id_type=MESH,
        )

    others(col, n_cols, lambda j: out_copy(j, col).start())
    out_recv[col] = out_send[:, col]
    others(col, n_cols, lambda j: out_copy(j, j).wait_recv())
    for which, out_ref in enumerate((solution_ref, residual_ref)):
        for block in range(blocks):
            lanes = pl.ds((block // 2) * 128, 128)
            for side in range(n_cols // 2):
                first = out_recv[2 * side, which, :, lanes]
                second = out_recv[2 * side + 1, which, :, lanes]
                low = half_lanes(first.shape)
                if block % 2 == 0:
                    joined = jnp.where(low, first, pltpu.roll(second, 64, 1))
                else:
                    joined = jnp.where(low, pltpu.roll(first, 64, 1), second)
                out_ref[:, pl.ds(block * 256 + side * 128, 128)] = joined

    others(col, n_cols, lambda j: item_copy(j).wait_send())
    others(col, n_cols, lambda j: user_copy(j).wait_send())
    others(own_a, GROUP, lambda j: gram_first(j, own_a).wait_send())
    others(own_b, GROUP, lambda j: gram_second(j, own_b).wait_send())
    others(own_a, GROUP, lambda j: gram_third(j, own_a).wait_send())
    others(col, n_cols, lambda j: out_copy(j, col).wait_send())


def conjugate(tables, user_factors, item_factors, tiles, tile_mask, n_cols):
    col_width, users = user_factors.shape
    slots, width, tile_cols = tiles.shape
    tile_rows = tile_mask.shape[1]
    blocks = users // tile_rows
    own_users = tile_rows // n_cols
    mine = blocks * own_users
    item_quarter = item_factors.shape[1] // n_cols
    vmem = pl.BlockSpec(memory_space=pltpu.VMEM)
    smem = pl.BlockSpec(memory_space=pltpu.SMEM)
    piece = width // GROUP
    out = jax.ShapeDtypeStruct((col_width, users), F32)
    return pl.pallas_call(
        cg_kernel,
        out_shape=(out, out),
        in_specs=[smem] * 6 + [vmem] * 3 + [pl.BlockSpec(memory_space=pl.ANY)],
        out_specs=(vmem, vmem),
        scratch_shapes=[
            pltpu.VMEM((slots, own_users, tile_cols), BF16),
            pltpu.VMEM((n_cols, col_width, mine), F32),
            pltpu.VMEM((width, mine), F32),
            pltpu.VMEM((width, item_quarter), BF16),
            pltpu.VMEM((GROUP, piece, width), F32),
            pltpu.VMEM((GROUP, piece, width), F32),
            pltpu.VMEM((piece, width), F32),
            pltpu.VMEM((GROUP, piece, width), F32),
            pltpu.VMEM((GROUP, piece, width), F32),
            pltpu.VMEM((4, 8, 128), F32),
            pltpu.VMEM((4, GROUP, 8, 128), F32),
            pltpu.VMEM((blocks, own_users, 2 * width), BF16),
            pltpu.VMEM((slots, own_users, width), F32),
            pltpu.VMEM((mine, width), F32),
            pltpu.VMEM((mine, width), F32),
            pltpu.VMEM((mine, width), F32),
            pltpu.VMEM((mine, width), F32),
            pltpu.VMEM((2, n_cols, col_width, mine), F32),
            pltpu.VMEM((n_cols, 2, col_width, mine), F32),
            pltpu.SemaphoreType.DMA,
            pltpu.SemaphoreType.DMA((n_cols,)),
            pltpu.SemaphoreType.DMA((n_cols,)),
            pltpu.SemaphoreType.DMA((n_cols,)),
            pltpu.SemaphoreType.DMA((n_cols,)),
            pltpu.SemaphoreType.DMA((3, GROUP)),
            pltpu.SemaphoreType.DMA((3, GROUP)),
            pltpu.SemaphoreType.DMA((4, GROUP)),
            pltpu.SemaphoreType.DMA((4, GROUP)),
            pltpu.SemaphoreType.DMA((n_cols,)),
            pltpu.SemaphoreType.DMA((n_cols,)),
        ],
        compiler_params=pltpu.CompilerParams(
            collective_id=0, has_side_effects=True, vmem_limit_bytes=VMEM_BYTES
        ),
    )(*tables, user_factors, item_factors, tiles, tile_mask)


def on_device(user_factors, item_factors, tile_user, tile_item, tile_count, tile_mask):
    n_rows, n_cols = lax.axis_size("rows"), lax.axis_size("cols")
    col_width = item_factors.shape[0]
    tile_rows = tile_mask.shape[1]
    slots = tile_user.shape[0]
    blocks = user_factors.shape[1] // tile_rows
    item_blocks = item_factors.shape[1] // tile_rows
    capacity = max(2, (slots + n_rows - 1) // n_rows)

    order = jnp.arange(slots, dtype=jnp.int32)
    live = order < tile_count[0]
    key = jnp.where(live, tile_user, blocks) * slots + order
    place = jnp.sum((key[None, :] < key[:, None]).astype(jnp.int32), axis=1)
    chosen = (place[None, :] == order[:, None]).astype(jnp.int32)
    perm = jnp.sum(chosen * order[None, :], axis=1)
    user = jnp.sum(chosen * tile_user[None, :], axis=1)
    live_sorted = live.astype(F32)
    keep = jnp.concatenate([jnp.zeros((1,), F32), (user[1:] == user[:-1]).astype(F32)])
    per_block = (user[None, :] == jnp.arange(blocks, dtype=jnp.int32)[:, None]) & live[None, :]
    has = jnp.any(per_block, axis=1).astype(F32)
    last = jnp.max(jnp.where(per_block, order[None, :], 0), axis=1)

    holder = tile_item // item_blocks
    earlier = (holder[None, :] == holder[:, None]) & (order[None, :] < order[:, None]) & live[None, :]
    rank = jnp.sum(earlier.astype(jnp.int32), axis=1)
    slot_ids = jnp.minimum(holder * capacity + rank, n_rows * capacity - 1)
    slot_range = jnp.arange(n_rows * capacity, dtype=jnp.int32)
    hits = ((slot_ids[None, :] == slot_range[:, None]) & live[None, :]).astype(jnp.int32)
    requests = jnp.sum(hits * (tile_item % item_blocks)[None, :], axis=1).reshape(n_rows, capacity)
    wanted = lax.all_to_all(requests, "rows", split_axis=0, concat_axis=0, tiled=True)
    shards = jnp.transpose(item_factors.reshape(col_width, item_blocks, tile_rows), (1, 0, 2))
    fetched = lax.all_to_all(shards[wanted], "rows", split_axis=0, concat_axis=0, tiled=True)
    slot_sorted = jnp.sum(chosen * slot_ids[None, :], axis=1)
    picked = fetched.reshape(n_rows * capacity, col_width, tile_rows)[slot_sorted]
    tiles = lax.all_gather(picked, "cols", axis=1, tiled=True)
    return conjugate(
        (perm, user, keep, live_sorted, last, has), user_factors, item_factors, tiles, tile_mask, n_cols
    )


def solution(mesh):
    return jax.shard_map(
        on_device,
        mesh=mesh,
        in_specs=(
            P("cols", "rows"),
            P("cols", "rows"),
            P("rows"),
            P("rows"),
            P("rows"),
            P("rows", None, None),
        ),
        out_specs=(P("cols", "rows"), P("cols", "rows")),
        check_vma=False,
    )
```

```python
import jax
import jax.numpy as jnp
from jax import lax
from jax.experimental import pallas as pl
from jax.experimental.pallas import tpu as pltpu
from jax.sharding import PartitionSpec as P

RIDGE = 0.5
CONFIDENCE = 40.0
HIGHEST = lax.Precision.HIGHEST
MESH = pl.DeviceIdType.MESH
F32 = jnp.float32
BF16 = jnp.bfloat16
Y_CHIPS = 4
Z_CHIPS = 8
CORES = 2
GROUP = 16
PLANE = Y_CHIPS * CORES
CAPACITY = 2
SLOTS = Z_CHIPS * CAPACITY
PIECES = 4
UNROLL = 24
VMEM_BYTES = 48 * 1024 * 1024


def interleave(first, second, odd):
    low = lax.broadcasted_iota(jnp.int32, first.shape, 1) < 64
    if odd:
        return jnp.where(low, pltpu.roll(first, 64, 1), second)
    return jnp.where(low, first, pltpu.roll(second, 64, 1))


def kernel(
    raw_ref, perm_ref, user_ref, keep_ref, live_ref, last_ref, has_ref,
    ask_ref, users_ref, items_ref, mask_ref,
    solution_ref, residual_ref,
    asked, asked_rows, asked_smem, ring_0, ring_1, ring_2, ring_3, plane_send,
    plane_recv_0, plane_recv_1, plane_recv_2, plane_recv_3, tiles, masks,
    users_send, users_recv, items_recv, gram_part, gram_recv, gram_piece, gram_all, gram,
    sums_send, sums_recv, halves, terms, state_x, state_r, state_d, image, out_send, out_recv,
    mask_sem, smem_sem, a_send, a_recv, z_send, z_recv, y_send, y_recv, x_send, x_recv,
    u_send, u_recv, i_send, i_recv, g_send, g_recv, s_send, s_recv, o_send, o_recv,
):
    rings = (ring_0, ring_1, ring_2, ring_3)
    plane_recvs = (plane_recv_0, plane_recv_1, plane_recv_2, plane_recv_3)
    row = lax.axis_index("rows")
    col = lax.axis_index("cols")
    n_cols = lax.axis_size("cols")
    core = lax.rem(row, CORES)
    own_z = lax.rem(lax.div(row, CORES), Z_CHIPS)
    own_y = lax.div(row, GROUP)
    own_a = lax.rem(row, GROUP)
    own_b = col * Y_CHIPS + own_y
    own_p = own_y * CORES + core
    tile_total, own_users, _ = masks.shape
    col_width = users_ref.shape[0]
    blocks = halves.shape[0]
    item_blocks = ring_0.shape[1]
    item_quarter = items_recv.shape[1]
    part = item_blocks // 2

    def peer_a(j):
        return (own_y * GROUP + j, col)

    def peer_b(j):
        return (lax.rem(j, Y_CHIPS) * GROUP + own_a, lax.div(j, Y_CHIPS))

    def peer_p(j):
        return (lax.div(j, CORES) * GROUP + own_z * CORES + lax.rem(j, CORES), col)

    def peer_c(j):
        return (row, j)

    z_peers = [
        (own_y * GROUP + lax.rem(own_z + step, Z_CHIPS) * CORES + core, col) for step in (1, Z_CHIPS - 1)
    ]
    right, left = lax.rem(col + 1, n_cols), lax.rem(col + n_cols - 1, n_cols)
    across = lax.rem(col + 2, n_cols)

    def others(own, count, body):
        def step(i, carry):
            body(lax.rem(own + i, count))
            return carry

        lax.fori_loop(1, count, step, 0)

    def remote(src, dst, send_sem, recv_sem, peer):
        return pltpu.make_async_remote_copy(
            src_ref=src, dst_ref=dst, send_sem=send_sem, recv_sem=recv_sem, device_id=peer, device_id_type=MESH
        )

    mask_copy = pltpu.make_async_copy(
        mask_ref.at[:, pl.ds(pl.multiple_of(col * own_users, own_users), own_users), :], masks, mask_sem
    )
    mask_copy.start()

    barrier = pltpu.get_barrier_semaphore()

    def greet(peer):
        pl.semaphore_signal(barrier, inc=1, device_id=peer, device_id_type=MESH)

    others(own_a, GROUP, lambda j: greet(peer_a(j)))
    others(own_b, GROUP, lambda j: greet(peer_b(j)))
    others(own_y, Y_CHIPS, lambda j: greet(peer_p(j * CORES + 1 - core)))

    def split_items(b, carry):
        block = items_ref[:, pl.ds(pl.multiple_of(b * 256, 256), 256)]
        for piece in range(PIECES):
            lane, sub = piece // 2, piece % 2
            rings[piece][0, b] = block[16 * sub : 16 * sub + 16, 128 * lane : 128 * lane + 128]
        return carry

    lax.fori_loop(0, item_blocks, split_items, 0, unroll=4)
    for dest in range(n_cols):
        for pair in range(blocks // 2):
            at = (dest // 2) * 128
            first = users_ref[:, pl.ds(2 * pair * 256 + at, 128)]
            second = users_ref[:, pl.ds((2 * pair + 1) * 256 + at, 128)]
            users_send[dest, :, pl.ds(pair * 128, 128)] = interleave(first, second, dest % 2 == 1)
    pl.semaphore_wait(barrier, 2 * (GROUP - 1) + Y_CHIPS - 1)

    def z_copy(piece, way, step, h):
        if way == 0:
            src, dst = (Z_CHIPS - step) % Z_CHIPS, Z_CHIPS - 1 - step
        else:
            src, dst = step, step + 1
        chunk = pl.ds(part * h, part)
        return remote(
            rings[piece].at[src, chunk], rings[piece].at[dst, chunk],
            z_send.at[piece, way, step, h], z_recv.at[piece, way, step, h], z_peers[way],
        )

    last_step = Z_CHIPS // 2 - 1

    def z_travels(step, way, h):
        return step < last_step or h == way

    def z_begin(piece):
        for h in range(2):
            for way in range(2):
                z_copy(piece, way, 0, h).start()

    def z_step(piece, step):
        for h in range(2):
            for way in range(2):
                z_copy(piece, way, step - 1, h).wait_recv()
                if z_travels(step, way, h):
                    z_copy(piece, way, step, h).start()

    def z_end(piece):
        for way in range(2):
            z_copy(piece, way, last_step, way).wait_recv()

    def ask_copy(j, slot):
        return remote(ask_ref.at[j], asked.at[slot], a_send.at[j], a_recv.at[slot], peer_p(j))

    def plane_copy(piece, j, slot):
        return remote(
            plane_send.at[piece, j], plane_recvs[piece].at[pl.ds(pl.multiple_of(slot * SLOTS, SLOTS), SLOTS)],
            y_send.at[piece, j], y_recv.at[piece, slot], peer_p(j),
        )

    def plane_begin(piece):
        def pick(j, carry):
            for slot in range(SLOTS):
                plane_send[piece, j, slot] = rings[piece][slot // CAPACITY, asked_smem[j, slot]]
            return carry

        lax.fori_loop(0, PLANE, pick, 0)
        others(own_p, PLANE, lambda j: plane_copy(piece, j, own_p).start())
        plane_recvs[piece][pl.ds(pl.multiple_of(own_p * SLOTS, SLOTS), SLOTS)] = plane_send[piece, own_p]

    def x_ref(piece, owner):
        rows_at = pl.multiple_of(owner * col_width + 16 * (piece % 2), 16)
        return tiles.at[piece // 2, :, pl.ds(rows_at, 16), :]

    def x_copy(piece, kind, owner, peer):
        return remote(
            x_ref(piece, owner), x_ref(piece, owner), x_send.at[piece, kind], x_recv.at[piece, kind], (row, peer)
        )

    def x_begin(piece):
        others(own_p, PLANE, lambda j: plane_copy(piece, j, j).wait_recv())
        rows_at = pl.multiple_of(col * col_width + 16 * (piece % 2), 16)

        def pack(s, carry):
            tiles[piece // 2, s, pl.ds(rows_at, 16), :] = plane_recvs[piece][raw_ref[s]]
            return carry

        lax.fori_loop(0, tile_total, pack, 0, unroll=8)
        x_copy(piece, 0, col, right).start()
        x_copy(piece, 1, col, left).start()

    def x_forward(piece):
        if piece % 2 == 0:
            x_copy(piece, 0, left, right).wait_recv()
            x_copy(piece, 2, left, right).start()
        else:
            x_copy(piece, 1, right, left).wait_recv()
            x_copy(piece, 2, right, left).start()

    def x_end(piece):
        if piece % 2 == 0:
            x_copy(piece, 1, right, left).wait_recv()
        else:
            x_copy(piece, 0, left, right).wait_recv()
        x_copy(piece, 2, across, left).wait_recv()

    own_cols = pl.ds(pl.multiple_of(col * col_width, col_width), col_width)

    def item_quarter_ref(j):
        return items_ref.at[:, pl.ds(pl.multiple_of(j * item_quarter, item_quarter), item_quarter)]

    def col_rows(j):
        return pl.ds(pl.multiple_of(j * col_width, col_width), col_width)

    def item_copy(j, slot):
        return remote(item_quarter_ref(j), items_recv.at[col_rows(slot)], i_send.at[j], i_recv.at[slot], peer_c(j))

    def user_copy(j, slot):
        return remote(users_send.at[j], users_recv.at[col_rows(slot)], u_send.at[j], u_recv.at[slot], peer_c(j))

    def gram_first(j, slot):
        return remote(gram_part.at[j], gram_recv.at[slot], g_send.at[0, j], g_recv.at[0, slot], peer_a(j))

    def gram_second(j, slot):
        return remote(gram_piece, gram_all.at[slot], g_send.at[1, j], g_recv.at[1, slot], peer_b(j))

    def gram_third(j, slot):
        return remote(gram.at[own_a], gram.at[slot], g_send.at[2, j], g_recv.at[2, slot], peer_a(j))

    def gram_1():
        others(col, n_cols, lambda j: item_copy(j, j).wait_recv())
        table = items_recv[...]
        gram_part[...] = lax.dot_general(
            table, table, (((1,), (1,)), ((), ())), preferred_element_type=F32
        ).reshape(gram_part.shape)
        others(own_a, GROUP, lambda j: gram_first(j, own_a).start())
        gram_recv[own_a] = gram_part[own_a]

    def gram_2():
        others(own_a, GROUP, lambda j: gram_first(j, j).wait_recv())
        gram_piece[...] = jnp.sum(gram_recv[...], axis=0)
        others(own_b, GROUP, lambda j: gram_second(j, own_b).start())
        gram_all[own_b] = gram_piece[...]

    def gram_3():
        others(own_b, GROUP, lambda j: gram_second(j, j).wait_recv())
        gram[own_a] = jnp.sum(gram_all[...], axis=0)
        others(own_a, GROUP, lambda j: gram_third(j, own_a).start())

    def sparse_part(vectors, lanes, first_time):
        high = vectors.astype(BF16)
        low = (vectors - high.astype(F32)).astype(BF16)
        halves[:, :own_users] = high.reshape(blocks, own_users, 128)
        halves[:, own_users:] = low.reshape(blocks, own_users, 128)

        def step(s, running):
            if len(lanes) == 2:
                item = jnp.concatenate([tiles[0, s], tiles[1, s]], axis=1)
                mask = masks[perm_ref[s]]
            else:
                item = tiles[lanes[0], s]
                mask = masks[perm_ref[s], :, pl.ds(128 * lanes[0], 128)]
            mask = mask.astype(F32) * live_ref[s]
            scores = jnp.dot(halves[user_ref[s]], item, preferred_element_type=F32)
            scores = scores[:own_users] + scores[own_users:]
            if first_time:
                strengths = mask * ((1.0 + CONFIDENCE) - CONFIDENCE * scores)
            else:
                strengths = mask * scores
            s_high = strengths.astype(BF16)
            s_low = (strengths - s_high.astype(F32)).astype(BF16)
            both = lax.dot_general(
                jnp.concatenate([s_high, s_low], axis=0), item, (((1,), (1,)), ((), ())),
                preferred_element_type=F32,
            )
            running = both[:own_users] + both[own_users:] + keep_ref[s] * running
            terms[s] = running
            return running

        lax.fori_loop(0, tile_total, step, jnp.zeros((own_users, 128), F32), unroll=UNROLL)
        return jnp.concatenate([terms[last_ref[b]] * has_ref[b] for b in range(blocks)], axis=0)

    def dense_part(vectors):
        return (
            jnp.dot(vectors, gram[...].reshape(128, 128), precision=HIGHEST, preferred_element_type=F32)
            + RIDGE * vectors
        )

    def sums_copy(at, peer, j, slot):
        return remote(sums_send.at[at], sums_recv.at[at, slot], s_send.at[at, j], s_recv.at[at, slot], peer(j))

    def all_sums(index, products):
        rows = [jnp.sum(p, axis=0, keepdims=True) for p in products]
        rows.append(jnp.zeros((8 - len(rows), 128), F32))
        total = jnp.concatenate(rows, axis=0)
        for stage, (peer, own) in enumerate(((peer_a, own_a), (peer_b, own_b))):
            at = 2 * index + stage
            sums_send[at] = total
            others(own, GROUP, lambda j: sums_copy(at, peer, j, own).start())
            sums_recv[at, own] = total
            others(own, GROUP, lambda j: sums_copy(at, peer, j, j).wait_recv())
            total = jnp.sum(sums_recv[at], axis=0)
        total = jnp.sum(total, axis=1, keepdims=True)
        return [total[i : i + 1, :] for i in range(len(products))]

    def out_copy(index, j, slot):
        return remote(
            out_send.at[index, j], out_recv.at[index, slot], o_send.at[index, j], o_recv.at[index, slot], peer_c(j)
        )

    def out_begin(index, vectors):
        out_send[index] = vectors.T.reshape(n_cols, col_width, blocks * own_users)
        others(col, n_cols, lambda j: out_copy(index, j, col).start())
        out_recv[index, col] = out_send[index, col]

    def out_end(index):
        others(col, n_cols, lambda j: out_copy(index, j, j).wait_recv())

    z_begin(0)
    others(own_p, PLANE, lambda j: ask_copy(j, own_p).start())
    asked[own_p] = ask_ref[own_p]
    others(col, n_cols, lambda j: item_copy(j, col).start())
    others(col, n_cols, lambda j: user_copy(j, col).start())
    items_recv[own_cols, :] = item_quarter_ref(col)[...]
    users_recv[own_cols, :] = users_send[col]

    others(own_p, PLANE, lambda j: ask_copy(j, j).wait_recv())
    asked_rows[...] = asked[:, 0, :]
    to_smem = pltpu.make_async_copy(asked_rows, asked_smem, smem_sem)
    to_smem.start()
    to_smem.wait()

    for piece in range(PIECES):
        z_step(piece, 1)
        if piece == 1:
            gram_2()
        if piece >= 2:
            x_forward(piece - 2)
        z_step(piece, 2)
        if piece == 0:
            gram_1()
        if piece >= 1:
            x_begin(piece - 1)
        z_step(piece, 3)
        if piece + 1 < PIECES:
            z_begin(piece + 1)
        z_end(piece)
        plane_begin(piece)
        if piece == 1:
            gram_3()
    x_forward(PIECES - 2)
    x_begin(PIECES - 1)
    others(col, n_cols, lambda j: user_copy(j, j).wait_recv())
    state_x[...] = users_recv[...].T
    mask_copy.wait()
    others(own_a, GROUP, lambda j: gram_third(j, j).wait_recv())
    x_end(0)
    x_end(1)
    state_r[...] = sparse_part(state_x[...], (0,), True) - dense_part(state_x[...])
    x_forward(PIECES - 1)
    x_end(2)
    x_end(3)

    state_r[...] += sparse_part(state_x[...], (1,), True)
    out_begin(0, state_r[...])
    image[...] = dense_part(state_r[...]) + CONFIDENCE * sparse_part(state_r[...], (0, 1), False)
    out_begin(1, image[...])
    norm_0, curve_0 = all_sums(0, [state_r[...] * state_r[...], state_r[...] * image[...]])
    alpha_0 = norm_0 / curve_0
    state_d[...] = state_r[...]
    state_r[...] = state_r[...] - alpha_0 * image[...]

    image_r = dense_part(state_r[...]) + CONFIDENCE * sparse_part(state_r[...], (0, 1), False)
    out_begin(2, image_r)
    norm_1, curve_rr, curve_rd, curve_dr = all_sums(
        1,
        [
            state_r[...] * state_r[...],
            state_r[...] * image_r,
            state_r[...] * image[...],
            state_d[...] * image_r,
        ],
    )
    beta = norm_1 / norm_0
    alpha_1 = norm_1 / (curve_rr + beta * (curve_rd + curve_dr) + beta * beta * curve_0)

    for index in range(3):
        out_end(index)
    for block in range(blocks):
        lanes = pl.ds((block // 2) * 128, 128)
        for side in range(n_cols // 2):
            start_r, image_d, image_1 = [
                interleave(out_recv[i, 2 * side, :, lanes], out_recv[i, 2 * side + 1, :, lanes], block % 2 == 1)
                for i in range(3)
            ]
            here = pl.ds(block * 256 + side * 128, 128)
            mid_r = start_r - alpha_0 * image_d
            mid_x = users_ref[:, here] + alpha_0 * start_r
            solution_ref[:, here] = mid_x + alpha_1 * (mid_r + beta * start_r)
            residual_ref[:, here] = mid_r - alpha_1 * (image_1 + beta * image_d)

    others(own_p, PLANE, lambda j: ask_copy(j, own_p).wait_send())
    others(col, n_cols, lambda j: item_copy(j, col).wait_send())
    others(col, n_cols, lambda j: user_copy(j, col).wait_send())
    others(own_a, GROUP, lambda j: gram_first(j, own_a).wait_send())
    others(own_b, GROUP, lambda j: gram_second(j, own_b).wait_send())
    others(own_a, GROUP, lambda j: gram_third(j, own_a).wait_send())
    for piece in range(PIECES):
        for step in range(last_step + 1):
            for way in range(2):
                for h in range(2):
                    if z_travels(step, way, h):
                        z_copy(piece, way, step, h).wait_send()
        others(own_p, PLANE, lambda j: plane_copy(piece, j, own_p).wait_send())
        x_copy(piece, 0, col, right).wait_send()
        x_copy(piece, 1, col, left).wait_send()
        x_copy(piece, 2, left, right).wait_send()
    for index in range(2):
        others(own_a, GROUP, lambda j: sums_copy(2 * index, peer_a, j, own_a).wait_send())
        others(own_b, GROUP, lambda j: sums_copy(2 * index + 1, peer_b, j, own_b).wait_send())
    for index in range(3):
        others(col, n_cols, lambda j: out_copy(index, j, col).wait_send())


def solve(tables, ask, user_factors, item_factors, tile_mask, n_cols):
    col_width, users = user_factors.shape
    slots, tile_rows, tile_cols = tile_mask.shape
    width = col_width * n_cols
    blocks = users // tile_rows
    item_blocks = item_factors.shape[1] // tile_rows
    own_users = tile_rows // n_cols
    mine = blocks * own_users
    item_quarter = item_factors.shape[1] // n_cols
    vmem = pl.BlockSpec(memory_space=pltpu.VMEM)
    smem = pl.BlockSpec(memory_space=pltpu.SMEM)
    piece = width // GROUP
    out = jax.ShapeDtypeStruct((col_width, users), F32)
    dma = pltpu.SemaphoreType.DMA
    return pl.pallas_call(
        kernel,
        out_shape=(out, out),
        in_specs=[smem] * 7 + [vmem] * 3 + [pl.BlockSpec(memory_space=pl.ANY)],
        out_specs=(vmem, vmem),
        scratch_shapes=[
            pltpu.VMEM((PLANE, 8, 128), jnp.int32),
            pltpu.VMEM((PLANE, 128), jnp.int32),
            pltpu.SMEM((PLANE, 128), jnp.int32),
            *[pltpu.VMEM((Z_CHIPS, item_blocks, 16, 128), BF16)] * PIECES,
            pltpu.VMEM((PIECES, PLANE, SLOTS, 16, 128), BF16),
            *[pltpu.VMEM((PLANE * SLOTS, 16, 128), BF16)] * PIECES,
            pltpu.VMEM((2, slots, width, 128), BF16),
            pltpu.VMEM((slots, own_users, tile_cols), BF16),
            pltpu.VMEM((n_cols, col_width, mine), F32),
            pltpu.VMEM((width, mine), F32),
            pltpu.VMEM((width, item_quarter), BF16),
            pltpu.VMEM((GROUP, piece, width), F32),
            pltpu.VMEM((GROUP, piece, width), F32),
            pltpu.VMEM((piece, width), F32),
            pltpu.VMEM((GROUP, piece, width), F32),
            pltpu.VMEM((GROUP, piece, width), F32),
            pltpu.VMEM((4, 8, 128), F32),
            pltpu.VMEM((4, GROUP, 8, 128), F32),
            pltpu.VMEM((blocks, 2 * own_users, width), BF16),
            pltpu.VMEM((slots, own_users, width), F32),
            pltpu.VMEM((mine, width), F32),
            pltpu.VMEM((mine, width), F32),
            pltpu.VMEM((mine, width), F32),
            pltpu.VMEM((mine, width), F32),
            pltpu.VMEM((3, n_cols, col_width, mine), F32),
            pltpu.VMEM((3, n_cols, col_width, mine), F32),
            dma,
            dma,
            dma((PLANE,)),
            dma((PLANE,)),
            dma((PIECES, 2, Z_CHIPS // 2, 2)),
            dma((PIECES, 2, Z_CHIPS // 2, 2)),
            dma((PIECES, PLANE)),
            dma((PIECES, PLANE)),
            dma((PIECES, 3)),
            dma((PIECES, 3)),
            dma((n_cols,)),
            dma((n_cols,)),
            dma((n_cols,)),
            dma((n_cols,)),
            dma((3, GROUP)),
            dma((3, GROUP)),
            dma((4, GROUP)),
            dma((4, GROUP)),
            dma((3, n_cols)),
            dma((3, n_cols)),
        ],
        compiler_params=pltpu.CompilerParams(
            collective_id=0, has_side_effects=True, vmem_limit_bytes=VMEM_BYTES
        ),
    )(*tables, ask, user_factors, item_factors, tile_mask)


def on_device(user_factors, item_factors, tile_user, tile_item, tile_count, tile_mask):
    n_cols = lax.axis_size("cols")
    tile_rows = tile_mask.shape[1]
    slots = tile_user.shape[0]
    blocks = user_factors.shape[1] // tile_rows
    item_blocks = item_factors.shape[1] // tile_rows
    own_z = lax.axis_index("rows") // CORES % Z_CHIPS

    order = jnp.arange(slots, dtype=jnp.int32)
    live = order < tile_count[0]
    key = jnp.where(live, tile_user, blocks) * slots + order
    place = jnp.sum((key[None, :] < key[:, None]).astype(jnp.int32), axis=1)
    chosen = (place[None, :] == order[:, None]).astype(jnp.int32)
    perm = jnp.sum(chosen * order[None, :], axis=1)
    user = jnp.sum(chosen * tile_user[None, :], axis=1)
    live_sorted = live.astype(F32)
    keep = jnp.concatenate([jnp.zeros((1,), F32), (user[1:] == user[:-1]).astype(F32)])
    per_block = (user[None, :] == jnp.arange(blocks, dtype=jnp.int32)[:, None]) & live[None, :]
    has = jnp.any(per_block, axis=1).astype(F32)
    last = jnp.max(jnp.where(per_block, order[None, :], 0), axis=1)

    holder = tile_item // item_blocks
    earlier = (holder[None, :] == holder[:, None]) & (order[None, :] < order[:, None]) & live[None, :]
    rank = jnp.minimum(jnp.sum(earlier.astype(jnp.int32), axis=1), CAPACITY - 1)
    peer = holder // GROUP * CORES + holder % CORES
    distance = (holder // CORES % Z_CHIPS - own_z + Z_CHIPS) % Z_CHIPS
    raw = jnp.where(live, peer * SLOTS + distance * CAPACITY + rank, 0)
    raw_range = jnp.arange(PLANE * SLOTS, dtype=jnp.int32)
    hits = ((raw[None, :] == raw_range[:, None]) & live[None, :]).astype(jnp.int32)
    ask = jnp.sum(hits * (tile_item % item_blocks)[None, :], axis=1).reshape(PLANE, 1, SLOTS)
    ask = jnp.pad(ask, ((0, 0), (0, 7), (0, 128 - SLOTS)))
    raw_sorted = jnp.sum(chosen * raw[None, :], axis=1)
    return solve(
        (raw_sorted, perm, user, keep, live_sorted, last, has), ask, user_factors, item_factors, tile_mask, n_cols
    )


def solution(mesh):
    return jax.shard_map(
        on_device,
        mesh=mesh,
        in_specs=(
            P("cols", "rows"),
            P("cols", "rows"),
            P("rows"),
            P("rows"),
            P("rows"),
            P("rows", None, None),
        ),
        out_specs=(P("cols", "rows"), P("cols", "rows")),
        check_vma=False,
    )
```

```python
import jax
import jax.numpy as jnp
from jax import lax
from jax.experimental import pallas as pl
from jax.experimental.pallas import tpu as pltpu
from jax.sharding import PartitionSpec as P

RIDGE = 0.5
CONFIDENCE = 40.0
HIGHEST = lax.Precision.HIGHEST
MESH = pl.DeviceIdType.MESH
F32 = jnp.float32
BF16 = jnp.bfloat16
Y_CHIPS = 4
Z_CHIPS = 8
CORES = 2
GROUP = 16
PLANE = Y_CHIPS * CORES
CAPACITY = 2
SLOTS = Z_CHIPS * CAPACITY
PIECES = 4
CHUNKS = 4
NEAR = SLOTS - CAPACITY
UNROLL = 24
VMEM_BYTES = 48 * 1024 * 1024


def interleave(first, second, odd):
    low = lax.broadcasted_iota(jnp.int32, first.shape, 1) < 64
    if odd:
        return jnp.where(low, pltpu.roll(first, 64, 1), second)
    return jnp.where(low, first, pltpu.roll(second, 64, 1))


def kernel(
    holder_ref, place_ref, perm_ref, user_ref, keep_ref, live_ref, last_ref, has_ref,
    ask_ref, users_ref, items_ref, mask_ref,
    solution_ref, residual_ref,
    asked, asked_rows, asked_smem, ring_0, ring_1, ring_2, ring_3, far_0, far_1, far_2, far_3, plane_send,
    plane_recv_0, plane_recv_1, plane_recv_2, plane_recv_3, tiles, masks,
    users_send, users_recv, items_recv, gram_part, gram_recv, gram_piece, gram_all, gram,
    sums_send, sums_recv, halves, terms, state_x, state_r, state_d, image, out_send, out_recv,
    mask_sem, smem_sem, a_send, a_recv, z_send, z_recv, y_send, y_recv, x_send, x_recv,
    u_send, u_recv, i_send, i_recv, g_send, g_recv, s_send, s_recv, o_send, o_recv,
):
    rings = (ring_0, ring_1, ring_2, ring_3)
    fars = (far_0, far_1, far_2, far_3)
    plane_recvs = (plane_recv_0, plane_recv_1, plane_recv_2, plane_recv_3)
    row = lax.axis_index("rows")
    col = lax.axis_index("cols")
    n_cols = lax.axis_size("cols")
    core = lax.rem(row, CORES)
    own_z = lax.rem(lax.div(row, CORES), Z_CHIPS)
    own_y = lax.div(row, GROUP)
    own_a = lax.rem(row, GROUP)
    own_b = col * Y_CHIPS + own_y
    own_p = own_y * CORES + core
    tile_total, own_users, _ = masks.shape
    col_width = users_ref.shape[0]
    blocks = halves.shape[0]
    item_blocks = ring_0.shape[1]
    item_quarter = items_recv.shape[1]
    part = item_blocks // CHUNKS

    def peer_a(j):
        return (own_y * GROUP + j, col)

    def peer_b(j):
        return (lax.rem(j, Y_CHIPS) * GROUP + own_a, lax.div(j, Y_CHIPS))

    def peer_p(j):
        return (lax.div(j, CORES) * GROUP + own_z * CORES + lax.rem(j, CORES), col)

    def peer_c(j):
        return (row, j)

    z_peers = [
        (own_y * GROUP + lax.rem(own_z + step, Z_CHIPS) * CORES + core, col) for step in (1, Z_CHIPS - 1)
    ]

    def others(own, count, body):
        def step(i, carry):
            body(lax.rem(own + i, count))
            return carry

        lax.fori_loop(1, count, step, 0)

    def remote(src, dst, send_sem, recv_sem, peer):
        return pltpu.make_async_remote_copy(
            src_ref=src, dst_ref=dst, send_sem=send_sem, recv_sem=recv_sem, device_id=peer, device_id_type=MESH
        )

    mask_copy = pltpu.make_async_copy(
        mask_ref.at[:, pl.ds(pl.multiple_of(col * own_users, own_users), own_users), :], masks, mask_sem
    )
    mask_copy.start()

    barrier = pltpu.get_barrier_semaphore()

    def greet(peer):
        pl.semaphore_signal(barrier, inc=1, device_id=peer, device_id_type=MESH)

    others(own_a, GROUP, lambda j: greet(peer_a(j)))
    others(own_b, GROUP, lambda j: greet(peer_b(j)))
    others(own_y, Y_CHIPS, lambda j: greet(peer_p(j * CORES + 1 - core)))

    def split_items(b, carry):
        block = items_ref[:, pl.ds(pl.multiple_of(b * 256, 256), 256)]
        for piece in range(PIECES):
            lane, sub = piece // 2, piece % 2
            rings[piece][0, b] = block[16 * sub : 16 * sub + 16, 128 * lane : 128 * lane + 128]
        return carry

    lax.fori_loop(0, item_blocks, split_items, 0, unroll=4)
    for dest in range(n_cols):
        for pair in range(blocks // 2):
            at = (dest // 2) * 128
            first = users_ref[:, pl.ds(2 * pair * 256 + at, 128)]
            second = users_ref[:, pl.ds((2 * pair + 1) * 256 + at, 128)]
            users_send[dest, :, pl.ds(pair * 128, 128)] = interleave(first, second, dest % 2 == 1)
    pl.semaphore_wait(barrier, 2 * (GROUP - 1) + Y_CHIPS - 1)

    def z_copy(piece, way, step, h):
        chunk = pl.ds(part * h, part)
        if way == 0:
            src = (Z_CHIPS - 1 - step) % (Z_CHIPS - 1)
            dst = Z_CHIPS - 2 - step
        else:
            src, dst = step, step + 1
        target = rings[piece].at[dst, chunk] if step < last_step else fars[piece].at[chunk]
        return remote(
            rings[piece].at[src, chunk], target,
            z_send.at[piece, way, step, h], z_recv.at[piece, way, step, h], z_peers[way],
        )

    last_step = Z_CHIPS // 2 - 1

    def z_travels(step, way, h):
        return step < last_step or (h < CHUNKS // 2) == (way == 0)

    def z_step(piece, step):
        for h in range(CHUNKS):
            for way in range(2):
                if step > 0 and z_travels(step - 1, way, h):
                    z_copy(piece, way, step - 1, h).wait_recv()
                if step <= last_step and z_travels(step, way, h):
                    z_copy(piece, way, step, h).start()

    def ask_copy(j, slot):
        return remote(ask_ref.at[j], asked.at[slot], a_send.at[j], a_recv.at[slot], peer_p(j))

    def plane_copy(piece, half, j, slot):
        first, count = ((0, NEAR), (NEAR, CAPACITY))[half]
        return remote(
            plane_send.at[piece, j, pl.ds(first, count)], plane_recvs[piece].at[slot, pl.ds(first, count)],
            y_send.at[piece, half, j], y_recv.at[piece, half, slot], peer_p(j),
        )

    def plane_begin(piece, half):
        first, count = ((0, NEAR), (NEAR, CAPACITY))[half]

        def pick(j, carry):
            for slot in range(first, first + count):
                if half == 0:
                    block = rings[piece][slot // CAPACITY, asked_smem[j, slot]]
                else:
                    block = fars[piece][asked_smem[j, slot]]
                plane_send[piece, j, slot] = block
            return carry

        lax.fori_loop(0, PLANE, pick, 0, unroll=2)
        others(own_p, PLANE, lambda j: plane_copy(piece, half, j, own_p).start())
        plane_recvs[piece][own_p, pl.ds(first, count)] = plane_send[piece, own_p, pl.ds(first, count)]

    def x_ref(piece, owner):
        rows_at = pl.multiple_of(owner * col_width + 16 * (piece % 2), 16)
        return tiles.at[piece // 2, :, pl.ds(rows_at, 16), :]

    def x_copy(piece, j, slot):
        return remote(
            x_ref(piece, slot), x_ref(piece, slot), x_send.at[piece, j], x_recv.at[piece, slot], peer_c(j)
        )

    def x_begin(piece):
        for half in range(2):
            others(own_p, PLANE, lambda j: plane_copy(piece, half, j, j).wait_recv())
        rows_at = pl.multiple_of(col * col_width + 16 * (piece % 2), 16)

        def pack(s, carry):
            tiles[piece // 2, s, pl.ds(rows_at, 16), :] = plane_recvs[piece][holder_ref[s], place_ref[s]]
            return carry

        lax.fori_loop(0, tile_total, pack, 0, unroll=8)
        others(col, n_cols, lambda j: x_copy(piece, j, col).start())

    def x_end(piece):
        others(col, n_cols, lambda j: x_copy(piece, j, j).wait_recv())

    own_cols = pl.ds(pl.multiple_of(col * col_width, col_width), col_width)

    def item_quarter_ref(j):
        return items_ref.at[:, pl.ds(pl.multiple_of(j * item_quarter, item_quarter), item_quarter)]

    def col_rows(j):
        return pl.ds(pl.multiple_of(j * col_width, col_width), col_width)

    def item_copy(j, slot):
        return remote(item_quarter_ref(j), items_recv.at[col_rows(slot)], i_send.at[j], i_recv.at[slot], peer_c(j))

    def user_copy(j, slot):
        return remote(users_send.at[j], users_recv.at[col_rows(slot)], u_send.at[j], u_recv.at[slot], peer_c(j))

    def gram_first(j, slot):
        return remote(gram_part.at[j], gram_recv.at[slot], g_send.at[0, j], g_recv.at[0, slot], peer_a(j))

    def gram_second(j, slot):
        return remote(gram_piece, gram_all.at[slot], g_send.at[1, j], g_recv.at[1, slot], peer_b(j))

    def gram_third(j, slot):
        return remote(gram.at[own_a], gram.at[slot], g_send.at[2, j], g_recv.at[2, slot], peer_a(j))

    def gram_1():
        others(col, n_cols, lambda j: item_copy(j, j).wait_recv())
        table = items_recv[...]
        gram_part[...] = lax.dot_general(
            table, table, (((1,), (1,)), ((), ())), preferred_element_type=F32
        ).reshape(gram_part.shape)
        others(own_a, GROUP, lambda j: gram_first(j, own_a).start())
        gram_recv[own_a] = gram_part[own_a]

    def gram_2():
        others(own_a, GROUP, lambda j: gram_first(j, j).wait_recv())
        gram_piece[...] = jnp.sum(gram_recv[...], axis=0)
        others(own_b, GROUP, lambda j: gram_second(j, own_b).start())
        gram_all[own_b] = gram_piece[...]

    def gram_3():
        others(own_b, GROUP, lambda j: gram_second(j, j).wait_recv())
        gram[own_a] = jnp.sum(gram_all[...], axis=0)
        others(own_a, GROUP, lambda j: gram_third(j, own_a).start())

    def sparse_part(vectors, lanes, first_time):
        high = vectors.astype(BF16)
        low = (vectors - high.astype(F32)).astype(BF16)
        halves[:, :own_users] = high.reshape(blocks, own_users, 128)
        halves[:, own_users:] = low.reshape(blocks, own_users, 128)

        def step(s, running):
            if len(lanes) == 2:
                item = jnp.concatenate([tiles[0, s], tiles[1, s]], axis=1)
                mask = masks[perm_ref[s]]
            else:
                item = tiles[lanes[0], s]
                mask = masks[perm_ref[s], :, pl.ds(128 * lanes[0], 128)]
            mask = mask.astype(F32) * live_ref[s]
            scores = jnp.dot(halves[user_ref[s]], item, preferred_element_type=F32)
            scores = scores[:own_users] + scores[own_users:]
            if first_time:
                strengths = mask * ((1.0 + CONFIDENCE) - CONFIDENCE * scores)
            else:
                strengths = mask * scores
            s_high = strengths.astype(BF16)
            s_low = (strengths - s_high.astype(F32)).astype(BF16)
            both = lax.dot_general(
                jnp.concatenate([s_high, s_low], axis=0), item, (((1,), (1,)), ((), ())),
                preferred_element_type=F32,
            )
            running = both[:own_users] + both[own_users:] + keep_ref[s] * running
            terms[s] = running
            return running

        lax.fori_loop(0, tile_total, step, jnp.zeros((own_users, 128), F32), unroll=UNROLL)
        return jnp.concatenate([terms[last_ref[b]] * has_ref[b] for b in range(blocks)], axis=0)

    def dense_part(vectors):
        return (
            jnp.dot(vectors, gram[...].reshape(128, 128), precision=HIGHEST, preferred_element_type=F32)
            + RIDGE * vectors
        )

    def sums_copy(at, peer, j, slot):
        return remote(sums_send.at[at], sums_recv.at[at, slot], s_send.at[at, j], s_recv.at[at, slot], peer(j))

    def all_sums(products):
        rows = [jnp.sum(p, axis=0, keepdims=True) for p in products]
        rows.append(jnp.zeros((8 - len(rows), 128), F32))
        total = jnp.sum(jnp.concatenate(rows, axis=0), axis=1, keepdims=True)
        at_lane = lax.broadcasted_iota(jnp.int32, (8, 128), 0) == lax.broadcasted_iota(jnp.int32, (8, 128), 1)
        total = jnp.sum(jnp.where(at_lane, total, 0.0), axis=0, keepdims=True)
        for at, (peer, own) in enumerate(((peer_a, own_a), (peer_b, own_b))):
            sums_send[at] = total
            others(own, GROUP, lambda j: sums_copy(at, peer, j, own).start())
            sums_recv[at, own] = total
            others(own, GROUP, lambda j: sums_copy(at, peer, j, j).wait_recv())
            total = jnp.sum(sums_recv[at], axis=0)
        return [total[:, i : i + 1] for i in range(len(products))]

    def out_copy(index, j, slot):
        return remote(
            out_send.at[index, j], out_recv.at[index, slot], o_send.at[index, j], o_recv.at[index, slot], peer_c(j)
        )

    def out_begin(index, vectors):
        out_send[index] = vectors.T.reshape(n_cols, col_width, blocks * own_users)
        others(col, n_cols, lambda j: out_copy(index, j, col).start())
        out_recv[index, col] = out_send[index, col]

    def out_end(index):
        others(col, n_cols, lambda j: out_copy(index, j, j).wait_recv())

    z_step(0, 0)
    others(own_p, PLANE, lambda j: ask_copy(j, own_p).start())
    asked[own_p] = ask_ref[own_p]
    others(col, n_cols, lambda j: item_copy(j, col).start())
    others(col, n_cols, lambda j: user_copy(j, col).start())
    items_recv[own_cols, :] = item_quarter_ref(col)[...]
    users_recv[own_cols, :] = users_send[col]

    others(own_p, PLANE, lambda j: ask_copy(j, j).wait_recv())
    asked_rows[...] = asked[:, 0, :]
    to_smem = pltpu.make_async_copy(asked_rows, asked_smem, smem_sem)
    to_smem.start()
    to_smem.wait()

    span = last_step + 2
    for time in range(1, 2 * (PIECES - 1) + span):
        for piece in range(PIECES):
            step = time - 2 * piece
            if 0 <= step < span:
                z_step(piece, step)
                if step == span - 2:
                    plane_begin(piece, 0)
                if step == span - 1:
                    plane_begin(piece, 1)
            if step == span:
                x_begin(piece)
        if time == 2:
            gram_1()
        if time == 4:
            gram_2()
        if time == 5:
            gram_3()
    others(col, n_cols, lambda j: user_copy(j, j).wait_recv())
    state_x[...] = users_recv[...].T
    mask_copy.wait()
    others(own_a, GROUP, lambda j: gram_third(j, j).wait_recv())
    x_begin(PIECES - 1)
    x_end(0)
    x_end(1)
    state_r[...] = sparse_part(state_x[...], (0,), True) - dense_part(state_x[...])
    x_end(2)
    x_end(3)

    state_r[...] += sparse_part(state_x[...], (1,), True)
    out_begin(0, state_r[...])
    image[...] = dense_part(state_r[...]) + CONFIDENCE * sparse_part(state_r[...], (0, 1), False)
    out_begin(1, image[...])

    full = gram[...].reshape(128, 128)
    diagonal = lax.broadcasted_iota(jnp.int32, full.shape, 0) == lax.broadcasted_iota(jnp.int32, full.shape, 1)
    trace = jnp.sum(jnp.sum(jnp.where(diagonal, full, 0.0), axis=0, keepdims=True), axis=1, keepdims=True)
    theta = 1.0 / (trace * (1.0 / 128) + RIDGE)
    state_d[...] = state_r[...] - theta * image[...]
    image_w = dense_part(state_d[...]) + CONFIDENCE * sparse_part(state_d[...], (0, 1), False)
    out_begin(2, image_w)
    rr, rw, ww, ri, wi, rj, wj = all_sums(
        [
            state_r[...] * state_r[...],
            state_r[...] * state_d[...],
            state_d[...] * state_d[...],
            state_r[...] * image[...],
            state_d[...] * image[...],
            state_r[...] * image_w,
            state_d[...] * image_w,
        ]
    )
    delta = rw / (rr - rw)
    more = 1.0 + delta
    alpha_0 = theta * more
    norm_1 = delta * delta * rr - 2.0 * delta * more * rw + more * more * ww
    beta = norm_1 / rr
    curve_1 = (
        more * more * wj
        - delta * more * (wi + rj)
        + delta * delta * ri
        + beta * (more * (wi + rj) - 2.0 * delta * ri)
        + beta * beta * ri
    )
    alpha_1 = norm_1 / curve_1

    for index in range(3):
        out_end(index)
    for block in range(blocks):
        lanes = pl.ds((block // 2) * 128, 128)
        for side in range(n_cols // 2):
            start_r, image_r, image_d = [
                interleave(out_recv[i, 2 * side, :, lanes], out_recv[i, 2 * side + 1, :, lanes], block % 2 == 1)
                for i in range(3)
            ]
            here = pl.ds(block * 256 + side * 128, 128)
            mid_r = more * (start_r - theta * image_r) - delta * start_r
            mid_x = users_ref[:, here] + alpha_0 * start_r
            solution_ref[:, here] = mid_x + alpha_1 * (mid_r + beta * start_r)
            residual_ref[:, here] = mid_r - alpha_1 * (more * image_d + (beta - delta) * image_r)

    others(own_p, PLANE, lambda j: ask_copy(j, own_p).wait_send())
    others(col, n_cols, lambda j: item_copy(j, col).wait_send())
    others(col, n_cols, lambda j: user_copy(j, col).wait_send())
    others(own_a, GROUP, lambda j: gram_first(j, own_a).wait_send())
    others(own_b, GROUP, lambda j: gram_second(j, own_b).wait_send())
    others(own_a, GROUP, lambda j: gram_third(j, own_a).wait_send())
    for piece in range(PIECES):
        for step in range(last_step + 1):
            for way in range(2):
                for h in range(CHUNKS):
                    if z_travels(step, way, h):
                        z_copy(piece, way, step, h).wait_send()
        for half in range(2):
            others(own_p, PLANE, lambda j: plane_copy(piece, half, j, own_p).wait_send())
        others(col, n_cols, lambda j: x_copy(piece, j, col).wait_send())
    others(own_a, GROUP, lambda j: sums_copy(0, peer_a, j, own_a).wait_send())
    others(own_b, GROUP, lambda j: sums_copy(1, peer_b, j, own_b).wait_send())
    for index in range(3):
        others(col, n_cols, lambda j: out_copy(index, j, col).wait_send())


def solve(tables, ask, user_factors, item_factors, tile_mask, n_cols):
    col_width, users = user_factors.shape
    slots, tile_rows, tile_cols = tile_mask.shape
    width = col_width * n_cols
    blocks = users // tile_rows
    item_blocks = item_factors.shape[1] // tile_rows
    own_users = tile_rows // n_cols
    mine = blocks * own_users
    item_quarter = item_factors.shape[1] // n_cols
    vmem = pl.BlockSpec(memory_space=pltpu.VMEM)
    smem = pl.BlockSpec(memory_space=pltpu.SMEM)
    piece = width // GROUP
    out = jax.ShapeDtypeStruct((col_width, users), F32)
    dma = pltpu.SemaphoreType.DMA
    return pl.pallas_call(
        kernel,
        out_shape=(out, out),
        in_specs=[smem] * 8 + [vmem] * 3 + [pl.BlockSpec(memory_space=pl.ANY)],
        out_specs=(vmem, vmem),
        scratch_shapes=[
            pltpu.VMEM((PLANE, 8, 128), jnp.int32),
            pltpu.VMEM((PLANE, 128), jnp.int32),
            pltpu.SMEM((PLANE, 128), jnp.int32),
            *[pltpu.VMEM((Z_CHIPS - 1, item_blocks, 16, 128), BF16)] * PIECES,
            *[pltpu.VMEM((item_blocks, 16, 128), BF16)] * PIECES,
            pltpu.VMEM((PIECES, PLANE, SLOTS, 16, 128), BF16),
            *[pltpu.VMEM((PLANE, SLOTS, 16, 128), BF16)] * PIECES,
            pltpu.VMEM((2, slots, width, 128), BF16),
            pltpu.VMEM((slots, own_users, tile_cols), BF16),
            pltpu.VMEM((n_cols, col_width, mine), F32),
            pltpu.VMEM((width, mine), F32),
            pltpu.VMEM((width, item_quarter), BF16),
            pltpu.VMEM((GROUP, piece, width), F32),
            pltpu.VMEM((GROUP, piece, width), F32),
            pltpu.VMEM((piece, width), F32),
            pltpu.VMEM((GROUP, piece, width), F32),
            pltpu.VMEM((GROUP, piece, width), F32),
            pltpu.VMEM((2, 1, 128), F32),
            pltpu.VMEM((2, GROUP, 1, 128), F32),
            pltpu.VMEM((blocks, 2 * own_users, width), BF16),
            pltpu.VMEM((slots, own_users, width), F32),
            pltpu.VMEM((mine, width), F32),
            pltpu.VMEM((mine, width), F32),
            pltpu.VMEM((mine, width), F32),
            pltpu.VMEM((mine, width), F32),
            pltpu.VMEM((3, n_cols, col_width, mine), F32),
            pltpu.VMEM((3, n_cols, col_width, mine), F32),
            dma,
            dma,
            dma((PLANE,)),
            dma((PLANE,)),
            dma((PIECES, 2, Z_CHIPS // 2, CHUNKS)),
            dma((PIECES, 2, Z_CHIPS // 2, CHUNKS)),
            dma((PIECES, 2, PLANE)),
            dma((PIECES, 2, PLANE)),
            dma((PIECES, n_cols)),
            dma((PIECES, n_cols)),
            dma((n_cols,)),
            dma((n_cols,)),
            dma((n_cols,)),
            dma((n_cols,)),
            dma((3, GROUP)),
            dma((3, GROUP)),
            dma((2, GROUP)),
            dma((2, GROUP)),
            dma((3, n_cols)),
            dma((3, n_cols)),
        ],
        compiler_params=pltpu.CompilerParams(
            collective_id=0, has_side_effects=True, vmem_limit_bytes=VMEM_BYTES
        ),
    )(*tables, ask, user_factors, item_factors, tile_mask)


def on_device(user_factors, item_factors, tile_user, tile_item, tile_count, tile_mask):
    n_cols = lax.axis_size("cols")
    tile_rows = tile_mask.shape[1]
    slots = tile_user.shape[0]
    blocks = user_factors.shape[1] // tile_rows
    item_blocks = item_factors.shape[1] // tile_rows
    own_z = lax.axis_index("rows") // CORES % Z_CHIPS

    order = jnp.arange(slots, dtype=jnp.int32)
    live = order < tile_count[0]
    key = jnp.where(live, tile_user, blocks) * slots + order
    place = jnp.sum((key[None, :] < key[:, None]).astype(jnp.int32), axis=1)
    chosen = (place[None, :] == order[:, None]).astype(jnp.int32)
    perm = jnp.sum(chosen * order[None, :], axis=1)
    user = jnp.sum(chosen * tile_user[None, :], axis=1)
    live_sorted = live.astype(F32)
    keep = jnp.concatenate([jnp.zeros((1,), F32), (user[1:] == user[:-1]).astype(F32)])
    per_block = (user[None, :] == jnp.arange(blocks, dtype=jnp.int32)[:, None]) & live[None, :]
    has = jnp.any(per_block, axis=1).astype(F32)
    last = jnp.max(jnp.where(per_block, order[None, :], 0), axis=1)

    holder = tile_item // item_blocks
    earlier = (holder[None, :] == holder[:, None]) & (order[None, :] < order[:, None]) & live[None, :]
    rank = jnp.minimum(jnp.sum(earlier.astype(jnp.int32), axis=1), CAPACITY - 1)
    peer = holder // GROUP * CORES + holder % CORES
    distance = (holder // CORES % Z_CHIPS - own_z + Z_CHIPS) % Z_CHIPS
    far = Z_CHIPS // 2
    distance = jnp.where(distance == far, Z_CHIPS - 1, distance - (distance > far).astype(jnp.int32))
    raw = jnp.where(live, peer * SLOTS + distance * CAPACITY + rank, 0)
    raw_range = jnp.arange(PLANE * SLOTS, dtype=jnp.int32)
    hits = ((raw[None, :] == raw_range[:, None]) & live[None, :]).astype(jnp.int32)
    ask = jnp.sum(hits * (tile_item % item_blocks)[None, :], axis=1).reshape(PLANE, 1, SLOTS)
    ask = jnp.pad(ask, ((0, 0), (0, 7), (0, 128 - SLOTS)))
    raw_sorted = jnp.sum(chosen * raw[None, :], axis=1)
    return solve(
        (raw_sorted // SLOTS, raw_sorted % SLOTS, perm, user, keep, live_sorted, last, has),
        ask, user_factors, item_factors, tile_mask, n_cols,
    )


def solution(mesh):
    return jax.shard_map(
        on_device,
        mesh=mesh,
        in_specs=(
            P("cols", "rows"),
            P("cols", "rows"),
            P("rows"),
            P("rows"),
            P("rows"),
            P("rows", None, None),
        ),
        out_specs=(P("cols", "rows"), P("cols", "rows")),
        check_vma=False,
    )
```

```python
import jax
import jax.numpy as jnp
from jax import lax
from jax.experimental import pallas as pl
from jax.experimental.pallas import tpu as pltpu
from jax.sharding import PartitionSpec as P

RIDGE = 0.5
CONFIDENCE = 40.0
HIGHEST = lax.Precision.HIGHEST
MESH = pl.DeviceIdType.MESH
F32 = jnp.float32
BF16 = jnp.bfloat16
Y_CHIPS = 4
Z_CHIPS = 8
CORES = 2
GROUP = 16
PLANE = Y_CHIPS * CORES
CAPACITY = 2
SLOTS = Z_CHIPS * CAPACITY
PIECES = 4
CHUNKS = 4
NEAR = SLOTS - CAPACITY
UNROLL = 24
VMEM_BYTES = 48 * 1024 * 1024


def interleave(first, second, odd):
    low = lax.broadcasted_iota(jnp.int32, first.shape, 1) < 64
    if odd:
        return jnp.where(low, pltpu.roll(first, 64, 1), second)
    return jnp.where(low, first, pltpu.roll(second, 64, 1))


def kernel(
    count_ref, user_in, item_in, users_in, items_in, mask_ref,
    solution_ref, residual_ref,
    users_ref, items_ref, user_col, item_col, table, table_smem, ask, asked, asked_rows, asked_smem, ring_0, ring_1, ring_2, ring_3, far_0, far_1, far_2, far_3, plane_send,
    plane_recv_0, plane_recv_1, plane_recv_2, plane_recv_3, tiles, masks,
    users_send, users_recv, items_recv, gram_part, gram_recv, gram_piece, gram_all, gram,
    sums_send, sums_recv, halves, terms, state_x, state_r, state_d, image, out_send, out_recv,
    users_sem, items_sem, mask_sem, smem_sem, table_sem, a_send, a_recv, z_send, z_recv, y_send, y_recv, x_send, x_recv,
    u_send, u_recv, i_send, i_recv, g_send, g_recv, s_send, s_recv, o_send, o_recv,
):
    rings = (ring_0, ring_1, ring_2, ring_3)
    fars = (far_0, far_1, far_2, far_3)
    plane_recvs = (plane_recv_0, plane_recv_1, plane_recv_2, plane_recv_3)
    row = lax.axis_index("rows")
    col = lax.axis_index("cols")
    n_cols = lax.axis_size("cols")
    core = lax.rem(row, CORES)
    own_z = lax.rem(lax.div(row, CORES), Z_CHIPS)
    own_y = lax.div(row, GROUP)
    own_a = lax.rem(row, GROUP)
    own_b = col * Y_CHIPS + own_y
    own_p = own_y * CORES + core
    tile_total, own_users, _ = masks.shape
    col_width = users_ref.shape[0]
    blocks = halves.shape[0]
    item_blocks = ring_0.shape[1]
    item_quarter = items_recv.shape[1]
    part = item_blocks // CHUNKS

    def peer_a(j):
        return (own_y * GROUP + j, col)

    def peer_b(j):
        return (lax.rem(j, Y_CHIPS) * GROUP + own_a, lax.div(j, Y_CHIPS))

    def peer_p(j):
        return (lax.div(j, CORES) * GROUP + own_z * CORES + lax.rem(j, CORES), col)

    def peer_c(j):
        return (row, j)

    z_peers = [
        (own_y * GROUP + lax.rem(own_z + step, Z_CHIPS) * CORES + core, col) for step in (1, Z_CHIPS - 1)
    ]

    right, left = lax.rem(col + 1, n_cols), lax.rem(col + n_cols - 1, n_cols)
    across = lax.rem(col + 2, n_cols)
    half_slots = tile_total // 2

    def others(own, count, body):
        def step(i, carry):
            body(lax.rem(own + i, count))
            return carry

        lax.fori_loop(1, count, step, 0)

    def remote(src, dst, send_sem, recv_sem, peer):
        return pltpu.make_async_remote_copy(
            src_ref=src, dst_ref=dst, send_sem=send_sem, recv_sem=recv_sem, device_id=peer, device_id_type=MESH
        )

    items_copy = pltpu.make_async_copy(items_in, items_ref, items_sem)
    users_copy = pltpu.make_async_copy(users_in, users_ref, users_sem)
    items_copy.start()
    users_copy.start()
    mask_copy = pltpu.make_async_copy(
        mask_ref.at[:, pl.ds(pl.multiple_of(col * own_users, own_users), own_users), :], masks, mask_sem
    )
    mask_copy.start()

    barrier = pltpu.get_barrier_semaphore()

    def greet(peer):
        pl.semaphore_signal(barrier, inc=1, device_id=peer, device_id_type=MESH)

    others(own_a, GROUP, lambda j: greet(peer_a(j)))
    others(own_b, GROUP, lambda j: greet(peer_b(j)))
    others(own_y, Y_CHIPS, lambda j: greet(peer_p(j * CORES + 1 - core)))

    def split_items(b, carry):
        block = items_ref[:, pl.ds(pl.multiple_of(b * 256, 256), 256)]
        for piece in range(PIECES):
            lane, sub = piece // 2, piece % 2
            rings[piece][0, b] = block[16 * sub : 16 * sub + 16, 128 * lane : 128 * lane + 128]
        return carry

    items_copy.wait()
    lax.fori_loop(0, item_blocks, split_items, 0, unroll=4)
    users_copy.wait()
    for dest in range(n_cols):
        for pair in range(blocks // 2):
            at = (dest // 2) * 128
            first = users_ref[:, pl.ds(2 * pair * 256 + at, 128)]
            second = users_ref[:, pl.ds((2 * pair + 1) * 256 + at, 128)]
            users_send[dest, :, pl.ds(pair * 128, 128)] = interleave(first, second, dest % 2 == 1)
    pl.semaphore_wait(barrier, 2 * (GROUP - 1) + Y_CHIPS - 1)

    def make_tables():
        user_col[...] = jnp.zeros_like(user_col)
        item_col[...] = jnp.zeros_like(item_col)

        def fill(t, carry):
            user_col[pl.ds(t, 1), :] = jnp.full((1, 128), user_in[t], jnp.int32)
            item_col[pl.ds(t, 1), :] = jnp.full((1, 128), item_in[t], jnp.int32)
            return carry

        lax.fori_loop(0, tile_total, fill, 0, unroll=8)
        square = user_col.shape
        down = lax.broadcasted_iota(jnp.int32, square, 0)
        over = lax.broadcasted_iota(jnp.int32, square, 1)
        count = count_ref[0]
        live = down < count
        users_down, items_down = user_col[...], item_col[...]

        def total(cond, value, axis):
            return jnp.sum(jnp.where(cond, value, 0), axis=axis, keepdims=True)

        key = jnp.where(live, users_down, blocks) * 128 + down
        place = total(key.T < key, 1, 1)
        chosen = place == over
        holder = items_down // item_blocks
        earlier = (holder.T == holder) & (over < down) & (over < count)
        rank = jnp.minimum(total(earlier, 1, 1), CAPACITY - 1)
        peer = holder // GROUP * CORES + holder % CORES
        distance = (holder // CORES % Z_CHIPS - own_z + Z_CHIPS) % Z_CHIPS
        far = Z_CHIPS // 2
        distance = jnp.where(distance == far, Z_CHIPS - 1, jnp.where(distance > far, distance - 1, distance))
        raw = jnp.where(live, peer * SLOTS + distance * CAPACITY + rank, 0)
        ask[...] = total((raw == over) & live, items_down % item_blocks, 0)
        user = total(chosen, users_down, 0)
        up_to = total(live & (users_down <= over), 1, 0)
        lane = over[:1]
        rows = [
            total(chosen, raw, 0),
            total(chosen, down, 0),
            user,
            jnp.where((user == pltpu.roll(user, 1, 1)) & (lane > 0), 1, 0),
            jnp.where(lane < count, 1, 0),
            jnp.maximum(up_to - 1, 0),
            total(live & (users_down == over), 1, 0),
            jnp.zeros_like(user),
        ]
        table[...] = jnp.concatenate(rows, axis=0)
        pltpu.make_async_copy(table, table_smem, table_sem).start()

    def z_copy(piece, way, step, h):
        chunk = pl.ds(part * h, part)
        if way == 0:
            src = (Z_CHIPS - 1 - step) % (Z_CHIPS - 1)
            dst = Z_CHIPS - 2 - step
        else:
            src, dst = step, step + 1
        target = rings[piece].at[dst, chunk] if step < last_step else fars[piece].at[chunk]
        return remote(
            rings[piece].at[src, chunk], target,
            z_send.at[piece, way, step, h], z_recv.at[piece, way, step, h], z_peers[way],
        )

    last_step = Z_CHIPS // 2 - 1

    def z_travels(step, way, h):
        return step < last_step or (h < CHUNKS // 2) == (way == 0)

    def z_step(piece, step):
        for h in range(CHUNKS):
            for way in range(2):
                if step > 0 and z_travels(step - 1, way, h):
                    z_copy(piece, way, step - 1, h).wait_recv()
                if step <= last_step and z_travels(step, way, h):
                    z_copy(piece, way, step, h).start()

    def ask_copy(j, slot):
        return remote(ask, asked.at[slot], a_send.at[j], a_recv.at[slot], peer_p(j))

    def plane_copy(piece, half, j, slot):
        first, count = ((0, NEAR), (NEAR, CAPACITY))[half]
        return remote(
            plane_send.at[piece, j, pl.ds(first, count)], plane_recvs[piece].at[slot, pl.ds(first, count)],
            y_send.at[piece, half, j], y_recv.at[piece, half, slot], peer_p(j),
        )

    def plane_begin(piece, half):
        first, count = ((0, NEAR), (NEAR, CAPACITY))[half]

        def pick(j, carry):
            for slot in range(first, first + count):
                if half == 0:
                    block = rings[piece][slot // CAPACITY, asked_smem[j, own_p * SLOTS + slot]]
                else:
                    block = fars[piece][asked_smem[j, own_p * SLOTS + slot]]
                plane_send[piece, j, slot] = block
            return carry

        lax.fori_loop(0, PLANE, pick, 0, unroll=2)
        others(own_p, PLANE, lambda j: plane_copy(piece, half, j, own_p).start())
        plane_recvs[piece][own_p, pl.ds(first, count)] = plane_send[piece, own_p, pl.ds(first, count)]

    def x_copy(piece, kind, owner, peer):
        half = (0, 1, 0, 1, 0, 1)[kind]
        rows_at = pl.multiple_of(owner * col_width + 16 * (piece % 2), 16)
        at = tiles.at[piece // 2, pl.ds(half * half_slots, half_slots), pl.ds(rows_at, 16), :]
        return remote(at, at, x_send.at[piece, kind], x_recv.at[piece, kind], (row, peer))

    def x_begin(piece):
        for half in range(2):
            others(own_p, PLANE, lambda j: plane_copy(piece, half, j, j).wait_recv())
        rows_at = pl.multiple_of(col * col_width + 16 * (piece % 2), 16)

        def pack(s, carry):
            raw = table_smem[0, s]
            tiles[piece // 2, s, pl.ds(rows_at, 16), :] = plane_recvs[piece][raw >> 4, raw & (SLOTS - 1)]
            return carry

        lax.fori_loop(0, tile_total, pack, 0, unroll=8)
        for kind, peer in ((0, right), (3, left), (1, right), (2, left)):
            x_copy(piece, kind, col, peer).start()

    def x_forward(piece):
        x_copy(piece, 0, left, right).wait_recv()
        x_copy(piece, 4, left, right).start()
        x_copy(piece, 3, right, left).wait_recv()
        x_copy(piece, 5, right, left).start()

    def x_end(piece):
        x_copy(piece, 1, left, right).wait_recv()
        x_copy(piece, 2, right, left).wait_recv()
        x_copy(piece, 4, across, left).wait_recv()
        x_copy(piece, 5, across, left).wait_recv()

    own_cols = pl.ds(pl.multiple_of(col * col_width, col_width), col_width)

    def item_quarter_ref(j):
        return items_ref.at[:, pl.ds(pl.multiple_of(j * item_quarter, item_quarter), item_quarter)]

    def col_rows(j):
        return pl.ds(pl.multiple_of(j * col_width, col_width), col_width)

    def item_copy(j, slot):
        return remote(item_quarter_ref(j), items_recv.at[col_rows(slot)], i_send.at[j], i_recv.at[slot], peer_c(j))

    def user_copy(j, slot):
        return remote(users_send.at[j], users_recv.at[col_rows(slot)], u_send.at[j], u_recv.at[slot], peer_c(j))

    def gram_first(j, slot):
        return remote(gram_part.at[j], gram_recv.at[slot], g_send.at[0, j], g_recv.at[0, slot], peer_a(j))

    def gram_second(j, slot):
        return remote(gram_piece, gram_all.at[slot], g_send.at[1, j], g_recv.at[1, slot], peer_b(j))

    def gram_third(j, slot):
        return remote(gram.at[own_a], gram.at[slot], g_send.at[2, j], g_recv.at[2, slot], peer_a(j))

    def gram_1():
        others(col, n_cols, lambda j: item_copy(j, j).wait_recv())
        table = items_recv[...]
        gram_part[...] = lax.dot_general(
            table, table, (((1,), (1,)), ((), ())), preferred_element_type=F32
        ).reshape(gram_part.shape)
        others(own_a, GROUP, lambda j: gram_first(j, own_a).start())
        gram_recv[own_a] = gram_part[own_a]

    def gram_2():
        others(own_a, GROUP, lambda j: gram_first(j, j).wait_recv())
        gram_piece[...] = jnp.sum(gram_recv[...], axis=0)
        others(own_b, GROUP, lambda j: gram_second(j, own_b).start())
        gram_all[own_b] = gram_piece[...]

    def gram_3():
        others(own_b, GROUP, lambda j: gram_second(j, j).wait_recv())
        gram[own_a] = jnp.sum(gram_all[...], axis=0)
        others(own_a, GROUP, lambda j: gram_third(j, own_a).start())

    def sparse_part(vectors, lanes, first_time):
        high = vectors.astype(BF16)
        low = (vectors - high.astype(F32)).astype(BF16)
        halves[:, :own_users] = high.reshape(blocks, own_users, 128)
        halves[:, own_users:] = low.reshape(blocks, own_users, 128)

        def step(s, running):
            if len(lanes) == 2:
                item = jnp.concatenate([tiles[0, s], tiles[1, s]], axis=1)
                mask = masks[table_smem[1, s]]
            else:
                item = tiles[lanes[0], s]
                mask = masks[table_smem[1, s], :, pl.ds(128 * lanes[0], 128)]
            mask = mask.astype(F32) * table_smem[4, s].astype(F32)
            scores = jnp.dot(halves[table_smem[2, s]], item, preferred_element_type=F32)
            scores = scores[:own_users] + scores[own_users:]
            if first_time:
                strengths = mask * ((1.0 + CONFIDENCE) - CONFIDENCE * scores)
            else:
                strengths = mask * scores
            s_high = strengths.astype(BF16)
            s_low = (strengths - s_high.astype(F32)).astype(BF16)
            both = lax.dot_general(
                jnp.concatenate([s_high, s_low], axis=0), item, (((1,), (1,)), ((), ())),
                preferred_element_type=F32,
            )
            running = both[:own_users] + both[own_users:] + table_smem[3, s].astype(F32) * running
            terms[s] = running
            return running

        lax.fori_loop(0, tile_total, step, jnp.zeros((own_users, 128), F32), unroll=UNROLL)
        return jnp.concatenate([jnp.where(table_smem[6, b] > 0, terms[table_smem[5, b]], 0.0) for b in range(blocks)], axis=0)

    def dense_part(vectors):
        return (
            jnp.dot(vectors, gram[...].reshape(128, 128), precision=HIGHEST, preferred_element_type=F32)
            + RIDGE * vectors
        )

    def sums_copy(at, peer, j, slot):
        return remote(sums_send.at[at], sums_recv.at[at, slot], s_send.at[at, j], s_recv.at[at, slot], peer(j))

    def all_sums(products):
        rows = [jnp.sum(p, axis=0, keepdims=True) for p in products]
        rows.append(jnp.zeros((8 - len(rows), 128), F32))
        total = jnp.sum(jnp.concatenate(rows, axis=0), axis=1, keepdims=True)
        at_lane = lax.broadcasted_iota(jnp.int32, (8, 128), 0) == lax.broadcasted_iota(jnp.int32, (8, 128), 1)
        total = jnp.sum(jnp.where(at_lane, total, 0.0), axis=0, keepdims=True)
        for at, (peer, own) in enumerate(((peer_a, own_a), (peer_b, own_b))):
            sums_send[at] = total
            others(own, GROUP, lambda j: sums_copy(at, peer, j, own).start())
            sums_recv[at, own] = total
            others(own, GROUP, lambda j: sums_copy(at, peer, j, j).wait_recv())
            total = jnp.sum(sums_recv[at], axis=0)
        return [total[:, i : i + 1] for i in range(len(products))]

    def out_copy(index, j, slot):
        return remote(
            out_send.at[index, j], out_recv.at[index, slot], o_send.at[index, j], o_recv.at[index, slot], peer_c(j)
        )

    def out_begin(index, vectors):
        out_send[index] = vectors.T.reshape(n_cols, col_width, blocks * own_users)
        others(col, n_cols, lambda j: out_copy(index, j, col).start())
        out_recv[index, col] = out_send[index, col]

    def out_end(index):
        others(col, n_cols, lambda j: out_copy(index, j, j).wait_recv())

    z_step(0, 0)
    make_tables()
    others(own_p, PLANE, lambda j: ask_copy(j, own_p).start())
    asked[own_p] = ask[...]
    others(col, n_cols, lambda j: item_copy(j, col).start())
    others(col, n_cols, lambda j: user_copy(j, col).start())
    items_recv[own_cols, :] = item_quarter_ref(col)[...]
    users_recv[own_cols, :] = users_send[col]

    others(own_p, PLANE, lambda j: ask_copy(j, j).wait_recv())
    asked_rows[...] = asked[:, 0, :]
    to_smem = pltpu.make_async_copy(asked_rows, asked_smem, smem_sem)
    to_smem.start()
    to_smem.wait()
    pltpu.make_async_copy(table, table_smem, table_sem).wait()

    span = last_step + 2
    for time in range(1, 2 * (PIECES - 1) + span):
        for piece in range(PIECES):
            step = time - 2 * piece
            if 0 <= step < span:
                z_step(piece, step)
                if step == span - 2:
                    plane_begin(piece, 0)
                if step == span - 1:
                    plane_begin(piece, 1)
            if step == span:
                x_begin(piece)
            if step == span + 1:
                x_forward(piece)
        if time == 2:
            gram_1()
        if time == 4:
            gram_2()
        if time == 5:
            gram_3()
    others(col, n_cols, lambda j: user_copy(j, j).wait_recv())
    state_x[...] = users_recv[...].T
    mask_copy.wait()
    others(own_a, GROUP, lambda j: gram_third(j, j).wait_recv())
    x_begin(PIECES - 1)
    x_end(0)
    x_end(1)
    state_r[...] = sparse_part(state_x[...], (0,), True) - dense_part(state_x[...])
    x_forward(PIECES - 1)
    x_end(2)
    x_end(3)

    state_r[...] += sparse_part(state_x[...], (1,), True)
    out_begin(0, state_r[...])
    image[...] = dense_part(state_r[...]) + CONFIDENCE * sparse_part(state_r[...], (0, 1), False)
    out_begin(1, image[...])

    full = gram[...].reshape(128, 128)
    diagonal = lax.broadcasted_iota(jnp.int32, full.shape, 0) == lax.broadcasted_iota(jnp.int32, full.shape, 1)
    trace = jnp.sum(jnp.sum(jnp.where(diagonal, full, 0.0), axis=0, keepdims=True), axis=1, keepdims=True)
    theta = 1.0 / (trace * (1.0 / 128) + RIDGE)
    state_d[...] = state_r[...] - theta * image[...]
    image_w = dense_part(state_d[...]) + CONFIDENCE * sparse_part(state_d[...], (0, 1), False)
    out_begin(2, image_w)
    rr, rw, ww, ri, wi, rj, wj = all_sums(
        [
            state_r[...] * state_r[...],
            state_r[...] * state_d[...],
            state_d[...] * state_d[...],
            state_r[...] * image[...],
            state_d[...] * image[...],
            state_r[...] * image_w,
            state_d[...] * image_w,
        ]
    )
    delta = rw / (rr - rw)
    more = 1.0 + delta
    alpha_0 = theta * more
    norm_1 = delta * delta * rr - 2.0 * delta * more * rw + more * more * ww
    beta = norm_1 / rr
    curve_1 = (
        more * more * wj
        - delta * more * (wi + rj)
        + delta * delta * ri
        + beta * (more * (wi + rj) - 2.0 * delta * ri)
        + beta * beta * ri
    )
    alpha_1 = norm_1 / curve_1

    for index in range(3):
        out_end(index)
    for block in range(blocks):
        lanes = pl.ds((block // 2) * 128, 128)
        for side in range(n_cols // 2):
            start_r, image_r, image_d = [
                interleave(out_recv[i, 2 * side, :, lanes], out_recv[i, 2 * side + 1, :, lanes], block % 2 == 1)
                for i in range(3)
            ]
            here = pl.ds(block * 256 + side * 128, 128)
            mid_r = more * (start_r - theta * image_r) - delta * start_r
            mid_x = users_ref[:, here] + alpha_0 * start_r
            solution_ref[:, here] = mid_x + alpha_1 * (mid_r + beta * start_r)
            residual_ref[:, here] = mid_r - alpha_1 * (more * image_d + (beta - delta) * image_r)

    others(own_p, PLANE, lambda j: ask_copy(j, own_p).wait_send())
    others(col, n_cols, lambda j: item_copy(j, col).wait_send())
    others(col, n_cols, lambda j: user_copy(j, col).wait_send())
    others(own_a, GROUP, lambda j: gram_first(j, own_a).wait_send())
    others(own_b, GROUP, lambda j: gram_second(j, own_b).wait_send())
    others(own_a, GROUP, lambda j: gram_third(j, own_a).wait_send())
    for piece in range(PIECES):
        for step in range(last_step + 1):
            for way in range(2):
                for h in range(CHUNKS):
                    if z_travels(step, way, h):
                        z_copy(piece, way, step, h).wait_send()
        for half in range(2):
            others(own_p, PLANE, lambda j: plane_copy(piece, half, j, own_p).wait_send())
        for kind, owner, peer in ((0, col, right), (1, col, right), (2, col, left), (3, col, left), (4, left, right), (5, right, left)):
            x_copy(piece, kind, owner, peer).wait_send()
    others(own_a, GROUP, lambda j: sums_copy(0, peer_a, j, own_a).wait_send())
    others(own_b, GROUP, lambda j: sums_copy(1, peer_b, j, own_b).wait_send())
    for index in range(3):
        others(col, n_cols, lambda j: out_copy(index, j, col).wait_send())


def on_device(user_factors, item_factors, tile_user, tile_item, tile_count, tile_mask):
    n_cols = lax.axis_size("cols")
    col_width, users = user_factors.shape
    slots, tile_rows, tile_cols = tile_mask.shape
    width = col_width * n_cols
    blocks = users // tile_rows
    item_blocks = item_factors.shape[1] // tile_rows
    own_users = tile_rows // n_cols
    mine = blocks * own_users
    item_quarter = item_factors.shape[1] // n_cols
    vmem = pl.BlockSpec(memory_space=pltpu.VMEM)
    smem = pl.BlockSpec(memory_space=pltpu.SMEM)
    hbm = pl.BlockSpec(memory_space=pl.ANY)
    piece = width // GROUP
    out = jax.ShapeDtypeStruct((col_width, users), F32)
    dma = pltpu.SemaphoreType.DMA
    return pl.pallas_call(
        kernel,
        out_shape=(out, out),
        in_specs=[smem] * 3 + [hbm] * 3,
        out_specs=(vmem, vmem),
        scratch_shapes=[
            pltpu.VMEM((col_width, users), F32),
            pltpu.VMEM((col_width, item_factors.shape[1]), BF16),
            pltpu.VMEM((128, 128), jnp.int32),
            pltpu.VMEM((128, 128), jnp.int32),
            pltpu.VMEM((8, 128), jnp.int32),
            pltpu.SMEM((8, 128), jnp.int32),
            pltpu.VMEM((1, 128), jnp.int32),
            pltpu.VMEM((PLANE, 1, 128), jnp.int32),
            pltpu.VMEM((PLANE, 128), jnp.int32),
            pltpu.SMEM((PLANE, 128), jnp.int32),
            *[pltpu.VMEM((Z_CHIPS - 1, item_blocks, 16, 128), BF16)] * PIECES,
            *[pltpu.VMEM((item_blocks, 16, 128), BF16)] * PIECES,
            pltpu.VMEM((PIECES, PLANE, SLOTS, 16, 128), BF16),
            *[pltpu.VMEM((PLANE, SLOTS, 16, 128), BF16)] * PIECES,
            pltpu.VMEM((2, slots, width, 128), BF16),
            pltpu.VMEM((slots, own_users, tile_cols), BF16),
            pltpu.VMEM((n_cols, col_width, mine), F32),
            pltpu.VMEM((width, mine), F32),
            pltpu.VMEM((width, item_quarter), BF16),
            pltpu.VMEM((GROUP, piece, width), F32),
            pltpu.VMEM((GROUP, piece, width), F32),
            pltpu.VMEM((piece, width), F32),
            pltpu.VMEM((GROUP, piece, width), F32),
            pltpu.VMEM((GROUP, piece, width), F32),
            pltpu.VMEM((2, 1, 128), F32),
            pltpu.VMEM((2, GROUP, 1, 128), F32),
            pltpu.VMEM((blocks, 2 * own_users, width), BF16),
            pltpu.VMEM((slots, own_users, width), F32),
            pltpu.VMEM((mine, width), F32),
            pltpu.VMEM((mine, width), F32),
            pltpu.VMEM((mine, width), F32),
            pltpu.VMEM((mine, width), F32),
            pltpu.VMEM((3, n_cols, col_width, mine), F32),
            pltpu.VMEM((3, n_cols, col_width, mine), F32),
            dma,
            dma,
            dma,
            dma,
            dma,
            dma((PLANE,)),
            dma((PLANE,)),
            dma((PIECES, 2, Z_CHIPS // 2, CHUNKS)),
            dma((PIECES, 2, Z_CHIPS // 2, CHUNKS)),
            dma((PIECES, 2, PLANE)),
            dma((PIECES, 2, PLANE)),
            dma((PIECES, 6)),
            dma((PIECES, 6)),
            dma((n_cols,)),
            dma((n_cols,)),
            dma((n_cols,)),
            dma((n_cols,)),
            dma((3, GROUP)),
            dma((3, GROUP)),
            dma((2, GROUP)),
            dma((2, GROUP)),
            dma((3, n_cols)),
            dma((3, n_cols)),
        ],
        compiler_params=pltpu.CompilerParams(
            collective_id=0, has_side_effects=True, vmem_limit_bytes=VMEM_BYTES
        ),
    )(tile_count, tile_user, tile_item, user_factors, item_factors, tile_mask)


def solution(mesh):
    return jax.shard_map(
        on_device,
        mesh=mesh,
        in_specs=(
            P("cols", "rows"),
            P("cols", "rows"),
            P("rows"),
            P("rows"),
            P("rows"),
            P("rows", None, None),
        ),
        out_specs=(P("cols", "rows"), P("cols", "rows")),
        check_vma=False,
    )
```

```python
import functools

import jax
import jax.numpy as jnp
from jax import lax
from jax.experimental import pallas as pl
from jax.experimental.pallas import tpu as pltpu
from jax.sharding import PartitionSpec as P

RIDGE = 0.5
CONFIDENCE = 40.0
HIGHEST = lax.Precision.HIGHEST
MESH = pl.DeviceIdType.MESH
F32 = jnp.float32
BF16 = jnp.bfloat16
Y_CHIPS = 4
Z_CHIPS = 8
CORES = 2
GROUP = 16
PLANE = Y_CHIPS * CORES
CAPACITY = 2
SLOTS = Z_CHIPS * CAPACITY
PIECES = 4
CHUNKS = 4
NEAR = SLOTS - CAPACITY
UNROLL = 36
VMEM_BYTES = 56 * 1024 * 1024
STARTS = (0, 2, 4, 6)
PACK_AFTER = -0.5
PASS_AFTER = 0.5


def interleave(first, second, odd):
    low = lax.broadcasted_iota(jnp.int32, first.shape, 1) < 64
    if odd:
        return jnp.where(low, pltpu.roll(first, 64, 1), second)
    return jnp.where(low, first, pltpu.roll(second, 64, 1))


def kernel(
    count_hbm, user_hbm, item_hbm, users_in, items_in, mask_ref,
    vectors_ref, scalars_ref,
    count_ref, user_in, item_in, users_ref, items_ref, user_col, item_col, table, table_smem, ask, asked, asked_rows, asked_smem, ring_0, ring_1, ring_2, ring_3, far_0, far_1, far_2, far_3, plane_send,
    plane_recv_0, plane_recv_1, plane_recv_2, plane_recv_3, tiles, masks,
    users_send, users_recv, items_recv, gram_part, gram_recv, gram_piece, gram_all, gram,
    sums_send, sums_recv, halves, terms, state_x, state_r, state_d, image, out_send, out_recv,
    lists_sem, users_sem, items_sem, mask_sem, smem_sem, table_sem, a_send, a_recv, z_send, z_recv, y_send, y_recv, x_send, x_recv,
    u_send, u_recv, i_send, i_recv, g_send, g_recv, s_send, s_recv, o_send, o_recv,
):
    rings = (ring_0, ring_1, ring_2, ring_3)
    fars = (far_0, far_1, far_2, far_3)
    plane_recvs = (plane_recv_0, plane_recv_1, plane_recv_2, plane_recv_3)
    row = lax.axis_index("rows")
    col = lax.axis_index("cols")
    n_cols = lax.axis_size("cols")
    core = lax.rem(row, CORES)
    own_z = lax.rem(lax.div(row, CORES), Z_CHIPS)
    own_y = lax.div(row, GROUP)
    own_a = lax.rem(row, GROUP)
    own_b = col * Y_CHIPS + own_y
    own_p = own_y * CORES + core
    tile_total, own_users, _ = masks.shape
    col_width = users_ref.shape[0]
    blocks = halves.shape[0]
    item_blocks = ring_0.shape[1]
    item_quarter = items_recv.shape[1]
    part = item_blocks // CHUNKS

    def peer_a(j):
        return (own_y * GROUP + j, col)

    def peer_b(j):
        return (lax.rem(j, Y_CHIPS) * GROUP + own_a, lax.div(j, Y_CHIPS))

    def peer_p(j):
        return (lax.div(j, CORES) * GROUP + own_z * CORES + lax.rem(j, CORES), col)

    def peer_c(j):
        return (row, j)

    z_peers = [
        (own_y * GROUP + lax.rem(own_z + step, Z_CHIPS) * CORES + core, col) for step in (1, Z_CHIPS - 1)
    ]

    right, left = lax.rem(col + 1, n_cols), lax.rem(col + n_cols - 1, n_cols)
    across = lax.rem(col + 2, n_cols)
    half_slots = tile_total // 2

    def others(own, count, body):
        def step(i, carry):
            body(lax.rem(own + i, count))
            return carry

        lax.fori_loop(1, count, step, 0)

    def remote(src, dst, send_sem, recv_sem, peer):
        return pltpu.make_async_remote_copy(
            src_ref=src, dst_ref=dst, send_sem=send_sem, recv_sem=recv_sem, device_id=peer, device_id_type=MESH
        )

    items_copy = pltpu.make_async_copy(items_in, items_ref, items_sem)
    users_copy = pltpu.make_async_copy(users_in, users_ref, users_sem)
    items_copy.start()
    users_copy.start()
    list_copies = [
        pltpu.make_async_copy(src, dst, lists_sem.at[i])
        for i, (src, dst) in enumerate(((count_hbm, count_ref), (user_hbm, user_in), (item_hbm, item_in)))
    ]
    for copy in list_copies:
        copy.start()
    mask_copy = pltpu.make_async_copy(
        mask_ref.at[:, pl.ds(pl.multiple_of(col * own_users, own_users), own_users), :], masks, mask_sem
    )

    barrier = pltpu.get_barrier_semaphore()

    def greet(peer):
        pl.semaphore_signal(barrier, inc=1, device_id=peer, device_id_type=MESH)

    for peer in z_peers:
        greet(peer)
    others(own_p, PLANE, lambda j: greet(peer_p(j)))
    others(col, n_cols, lambda j: greet(peer_c(j)))

    def split_items(b, carry):
        block = items_ref[:, pl.ds(pl.multiple_of(b * 256, 256), 256)]
        for piece in range(PIECES):
            lane, sub = piece // 2, piece % 2
            rings[piece][0, b] = block[16 * sub : 16 * sub + 16, 128 * lane : 128 * lane + 128]
        return carry

    items_copy.wait()
    lax.fori_loop(0, item_blocks, split_items, 0, unroll=4)
    def make_tables():
        user_col[...] = jnp.zeros_like(user_col)
        item_col[...] = jnp.zeros_like(item_col)

        def fill(t, carry):
            user_col[pl.ds(t, 1), :] = jnp.full((1, 128), user_in[t], jnp.int32)
            item_col[pl.ds(t, 1), :] = jnp.full((1, 128), item_in[t], jnp.int32)
            return carry

        lax.fori_loop(0, tile_total, fill, 0, unroll=8)
        square = user_col.shape
        down = lax.broadcasted_iota(jnp.int32, square, 0)
        over = lax.broadcasted_iota(jnp.int32, square, 1)
        count = count_ref[0]
        live = down < count
        users_down, items_down = user_col[...], item_col[...]

        def total(cond, value, axis):
            return jnp.sum(jnp.where(cond, value, 0), axis=axis, keepdims=True)

        key = jnp.where(live, users_down, blocks) * 128 + down
        place = total(key.T < key, 1, 1)
        chosen = place == over
        holder = items_down // item_blocks
        earlier = (holder.T == holder) & (over < down) & (over < count)
        rank = jnp.minimum(total(earlier, 1, 1), CAPACITY - 1)
        peer = holder // GROUP * CORES + holder % CORES
        distance = (holder // CORES % Z_CHIPS - own_z + Z_CHIPS) % Z_CHIPS
        far = Z_CHIPS // 2
        distance = jnp.where(distance == far, Z_CHIPS - 1, jnp.where(distance > far, distance - 1, distance))
        raw = jnp.where(live, peer * SLOTS + distance * CAPACITY + rank, 0)
        ask[...] = total((raw == over) & live, items_down % item_blocks, 0)
        user = total(chosen, users_down, 0)
        up_to = total(live & (users_down <= over), 1, 0)
        lane = over[:1]
        rows = [
            total(chosen, raw, 0),
            total(chosen, down, 0),
            user,
            jnp.where((user == pltpu.roll(user, 1, 1)) & (lane > 0), 1, 0),
            jnp.where(lane < count, 1, 0),
            jnp.maximum(up_to - 1, 0),
            total(live & (users_down == over), 1, 0),
            jnp.zeros_like(user),
        ]
        table[...] = jnp.concatenate(rows, axis=0)
        pltpu.make_async_copy(table, table_smem, table_sem).start()

    for copy in list_copies:
        copy.wait()
    make_tables()
    users_copy.wait()
    for dest in range(n_cols):
        for pair in range(blocks // 2):
            at = (dest // 2) * 128
            first = users_ref[:, pl.ds(2 * pair * 256 + at, 128)]
            second = users_ref[:, pl.ds((2 * pair + 1) * 256 + at, 128)]
            users_send[dest, :, pl.ds(pair * 128, 128)] = interleave(first, second, dest % 2 == 1)
    pl.semaphore_wait(barrier, 2 + PLANE - 1 + n_cols - 1)

    def z_copy(piece, way, step, h):
        chunk = pl.ds(part * h, part)
        if way == 0:
            src = (Z_CHIPS - 1 - step) % (Z_CHIPS - 1)
            dst = Z_CHIPS - 2 - step
        else:
            src, dst = step, step + 1
        target = rings[piece].at[dst, chunk] if step < last_step else fars[piece].at[chunk]
        return remote(
            rings[piece].at[src, chunk], target,
            z_send.at[piece, way, step, h], z_recv.at[piece, way, step, h], z_peers[way],
        )

    last_step = Z_CHIPS // 2 - 1

    def z_travels(step, way, h):
        return step < last_step or (h < CHUNKS // 2) == (way == 0)

    def z_step(piece, step):
        for h in range(CHUNKS):
            for way in range(2):
                if step > 0 and z_travels(step - 1, way, h):
                    z_copy(piece, way, step - 1, h).wait_recv()
                if step <= last_step and z_travels(step, way, h):
                    z_copy(piece, way, step, h).start()

    def ask_copy(j, slot):
        return remote(ask, asked.at[slot], a_send.at[j], a_recv.at[slot], peer_p(j))

    def plane_copy(piece, half, j, slot):
        first, count = ((0, NEAR), (NEAR, CAPACITY))[half]
        return remote(
            plane_send.at[piece, j, pl.ds(first, count)], plane_recvs[piece].at[slot, pl.ds(first, count)],
            y_send.at[piece, half, j], y_recv.at[piece, half, slot], peer_p(j),
        )

    def plane_begin(piece, half):
        first, count = ((0, NEAR), (NEAR, CAPACITY))[half]

        def pick(j, carry):
            for slot in range(first, first + count):
                if half == 0:
                    block = rings[piece][slot // CAPACITY, asked_smem[j, own_p * SLOTS + slot]]
                else:
                    block = fars[piece][asked_smem[j, own_p * SLOTS + slot]]
                plane_send[piece, j, slot] = block
            return carry

        lax.fori_loop(0, PLANE, pick, 0, unroll=2)
        others(own_p, PLANE, lambda j: plane_copy(piece, half, j, own_p).start())
        plane_recvs[piece][own_p, pl.ds(first, count)] = plane_send[piece, own_p, pl.ds(first, count)]

    def x_copy(piece, kind, owner, peer):
        half = (0, 1, 0, 1, 0, 1)[kind]
        rows_at = pl.multiple_of(owner * col_width + 16 * (piece % 2), 16)
        at = tiles.at[piece // 2, pl.ds(half * half_slots, half_slots), pl.ds(rows_at, 16), :]
        return remote(at, at, x_send.at[piece, kind], x_recv.at[piece, kind], (row, peer))

    def x_begin(piece):
        for half in range(2):
            others(own_p, PLANE, lambda j: plane_copy(piece, half, j, j).wait_recv())
        rows_at = pl.multiple_of(col * col_width + 16 * (piece % 2), 16)

        def pack(s, carry):
            raw = table_smem[0, s]
            tiles[piece // 2, s, pl.ds(rows_at, 16), :] = plane_recvs[piece][raw >> 4, raw & (SLOTS - 1)]
            return carry

        lax.fori_loop(0, tile_total, pack, 0, unroll=8)
        for kind, peer in ((0, right), (3, left), (1, right), (2, left)):
            x_copy(piece, kind, col, peer).start()

    def x_forward(piece):
        x_copy(piece, 0, left, right).wait_recv()
        x_copy(piece, 4, left, right).start()
        x_copy(piece, 3, right, left).wait_recv()
        x_copy(piece, 5, right, left).start()

    def x_end(piece):
        x_copy(piece, 1, left, right).wait_recv()
        x_copy(piece, 2, right, left).wait_recv()
        x_copy(piece, 4, across, left).wait_recv()
        x_copy(piece, 5, across, left).wait_recv()

    own_cols = pl.ds(pl.multiple_of(col * col_width, col_width), col_width)

    def item_quarter_ref(j):
        return items_ref.at[:, pl.ds(pl.multiple_of(j * item_quarter, item_quarter), item_quarter)]

    def col_rows(j):
        return pl.ds(pl.multiple_of(j * col_width, col_width), col_width)

    def item_copy(j, slot):
        return remote(item_quarter_ref(j), items_recv.at[col_rows(slot)], i_send.at[j], i_recv.at[slot], peer_c(j))

    def user_copy(j, slot):
        return remote(users_send.at[j], users_recv.at[col_rows(slot)], u_send.at[j], u_recv.at[slot], peer_c(j))

    def gram_first(j, slot):
        return remote(gram_part.at[j], gram_recv.at[slot], g_send.at[0, j], g_recv.at[0, slot], peer_a(j))

    def gram_second(j, slot):
        return remote(gram_piece, gram_all.at[slot], g_send.at[1, j], g_recv.at[1, slot], peer_b(j))

    def gram_third(j, slot):
        return remote(gram.at[own_a], gram.at[slot], g_send.at[2, j], g_recv.at[2, slot], peer_a(j))

    def gram_1():
        others(col, n_cols, lambda j: item_copy(j, j).wait_recv())
        table = items_recv[...]
        gram_part[...] = lax.dot_general(
            table, table, (((1,), (1,)), ((), ())), preferred_element_type=F32
        ).reshape(gram_part.shape)
        others(own_a, GROUP, lambda j: gram_first(j, own_a).start())
        gram_recv[own_a] = gram_part[own_a]

    def gram_2():
        others(own_a, GROUP, lambda j: gram_first(j, j).wait_recv())
        gram_piece[...] = jnp.sum(gram_recv[...], axis=0)
        others(own_b, GROUP, lambda j: gram_second(j, own_b).start())
        gram_all[own_b] = gram_piece[...]

    def gram_3():
        others(own_b, GROUP, lambda j: gram_second(j, j).wait_recv())
        gram[own_a] = jnp.sum(gram_all[...], axis=0)
        others(own_a, GROUP, lambda j: gram_third(j, own_a).start())

    def sparse_part(vectors, lanes, first_time):
        high = vectors.astype(BF16)
        low = (vectors - high.astype(F32)).astype(BF16)
        halves[:, :own_users] = high.reshape(blocks, own_users, 128)
        halves[:, own_users:] = low.reshape(blocks, own_users, 128)

        def step(s, running):
            if len(lanes) == 2:
                item = jnp.concatenate([tiles[0, s], tiles[1, s]], axis=1)
                mask = masks[table_smem[1, s]]
            else:
                item = tiles[lanes[0], s]
                mask = masks[table_smem[1, s], :, pl.ds(128 * lanes[0], 128)]
            mask = mask.astype(F32) * table_smem[4, s].astype(F32)
            scores = jnp.dot(halves[table_smem[2, s]], item, preferred_element_type=F32)
            scores = scores[:own_users] + scores[own_users:]
            if first_time:
                strengths = mask * ((1.0 + CONFIDENCE) - CONFIDENCE * scores)
            else:
                strengths = mask * scores
            s_high = strengths.astype(BF16)
            s_low = (strengths - s_high.astype(F32)).astype(BF16)
            both = lax.dot_general(
                jnp.concatenate([s_high, s_low], axis=0), item, (((1,), (1,)), ((), ())),
                preferred_element_type=F32,
            )
            running = both[:own_users] + both[own_users:] + table_smem[3, s].astype(F32) * running
            terms[s] = running
            return running

        lax.fori_loop(0, tile_total, step, jnp.zeros((own_users, 128), F32), unroll=UNROLL)
        return jnp.concatenate([jnp.where(table_smem[6, b] > 0, terms[table_smem[5, b]], 0.0) for b in range(blocks)], axis=0)

    def dense_part(vectors):
        return (
            jnp.dot(vectors, gram[...].reshape(128, 128), precision=HIGHEST, preferred_element_type=F32)
            + RIDGE * vectors
        )

    def sums_copy(at, peer, j, slot):
        return remote(sums_send.at[at], sums_recv.at[at, slot], s_send.at[at, j], s_recv.at[at, slot], peer(j))

    def all_sums(products):
        rows = [jnp.sum(p, axis=0, keepdims=True) for p in products]
        rows.append(jnp.zeros((8 - len(rows), 128), F32))
        total = jnp.sum(jnp.concatenate(rows, axis=0), axis=1, keepdims=True)
        at_lane = lax.broadcasted_iota(jnp.int32, (8, 128), 0) == lax.broadcasted_iota(jnp.int32, (8, 128), 1)
        total = jnp.sum(jnp.where(at_lane, total, 0.0), axis=0, keepdims=True)
        for at, (peer, own) in enumerate(((peer_a, own_a), (peer_b, own_b))):
            sums_send[at] = total
            others(own, GROUP, lambda j: sums_copy(at, peer, j, own).start())
            sums_recv[at, own] = total
            others(own, GROUP, lambda j: sums_copy(at, peer, j, j).wait_recv())
            total = jnp.sum(sums_recv[at], axis=0)
        return [total[:, i : i + 1] for i in range(len(products))]

    def out_copy(index, j, slot):
        return remote(
            out_send.at[index, j], out_recv.at[index, slot], o_send.at[index, j], o_recv.at[index, slot], peer_c(j)
        )

    def out_begin(index, vectors):
        out_send[index] = vectors.T.reshape(n_cols, col_width, blocks * own_users)
        others(col, n_cols, lambda j: out_copy(index, j, col).start())
        out_recv[index, col] = out_send[index, col]

    def out_end(index):
        others(col, n_cols, lambda j: out_copy(index, j, j).wait_recv())

    z_step(0, 0)
    mask_copy.start()
    others(own_p, PLANE, lambda j: ask_copy(j, own_p).start())
    asked[own_p] = ask[...]
    others(col, n_cols, lambda j: item_copy(j, col).start())
    z_step(0, 1)
    others(col, n_cols, lambda j: user_copy(j, col).start())
    items_recv[own_cols, :] = item_quarter_ref(col)[...]
    users_recv[own_cols, :] = users_send[col]

    def asked_ready():
        others(own_p, PLANE, lambda j: ask_copy(j, j).wait_recv())
        asked_rows[...] = asked[:, 0, :]
        to_smem = pltpu.make_async_copy(asked_rows, asked_smem, smem_sem)
        to_smem.start()
        to_smem.wait()
        pltpu.make_async_copy(table, table_smem, table_sem).wait()

    span = last_step + 2
    def first_half():
        others(col, n_cols, lambda j: user_copy(j, j).wait_recv())
        state_x[...] = users_recv[...].T
        mask_copy.wait()
        others(own_a, GROUP, lambda j: gram_third(j, j).wait_recv())
        x_end(1)
        state_r[...] = sparse_part(state_x[...], (0,), True) - dense_part(state_x[...])

    def gram_middle():
        x_end(0)
        gram_2()

    events = []
    for piece, start in enumerate(STARTS):
        for step in range(span):
            if (piece, step) not in ((0, 0), (0, 1)):
                events.append((start + step, functools.partial(z_step, piece, step)))
            if step == span - 2:
                if piece == 0:
                    events.append((start + step, asked_ready))
                events.append((start + step, functools.partial(plane_begin, piece, 0)))
            if step == span - 1:
                events.append((start + step, functools.partial(plane_begin, piece, 1)))
        events.append((start + span + PACK_AFTER, functools.partial(x_begin, piece)))
        events.append((start + span + PASS_AFTER, functools.partial(x_forward, piece)))
    events.append((STARTS[0] + span, gram_1))
    events.append((STARTS[0] + span + 2, gram_middle))
    events.append((STARTS[-1] + span, gram_3))
    events.append((STARTS[-1] + span, first_half))
    for _, event in sorted(events, key=lambda item: item[0]):
        event()
    x_end(2)
    x_end(3)

    state_r[...] += sparse_part(state_x[...], (1,), True)
    out_begin(0, state_r[...])
    image[...] = dense_part(state_r[...]) + CONFIDENCE * sparse_part(state_r[...], (0, 1), False)
    out_begin(1, image[...])

    full = gram[...].reshape(128, 128)
    diagonal = lax.broadcasted_iota(jnp.int32, full.shape, 0) == lax.broadcasted_iota(jnp.int32, full.shape, 1)
    trace = jnp.sum(jnp.sum(jnp.where(diagonal, full, 0.0), axis=0, keepdims=True), axis=1, keepdims=True)
    theta = 1.0 / (trace * (1.0 / 128) + RIDGE)
    state_d[...] = state_r[...] - theta * image[...]
    image_w = dense_part(state_d[...]) + CONFIDENCE * sparse_part(state_d[...], (0, 1), False)
    out_begin(2, image_w)
    rr, rw, ww, ri, wi, rj, wj = all_sums(
        [
            state_r[...] * state_r[...],
            state_r[...] * state_d[...],
            state_d[...] * state_d[...],
            state_r[...] * image[...],
            state_d[...] * image[...],
            state_r[...] * image_w,
            state_d[...] * image_w,
        ]
    )
    delta = rw / (rr - rw)
    more = 1.0 + delta
    alpha_0 = theta * more
    norm_1 = delta * delta * rr - 2.0 * delta * more * rw + more * more * ww
    beta = norm_1 / rr
    curve_1 = (
        more * more * wj
        - delta * more * (wi + rj)
        + delta * delta * ri
        + beta * (more * (wi + rj) - 2.0 * delta * ri)
        + beta * beta * ri
    )
    alpha_1 = norm_1 / curve_1

    for index in range(3):
        out_end(index)
    for block in range(blocks):
        lanes = pl.ds((block // 2) * 128, 128)
        for side in range(n_cols // 2):
            here = pl.ds(block * 256 + side * 128, 128)
            for i in range(3):
                vectors_ref[i, :, here] = interleave(
                    out_recv[i, 2 * side, :, lanes], out_recv[i, 2 * side + 1, :, lanes], block % 2 == 1
                )
    for i, value in enumerate((theta, delta, alpha_0, alpha_1, beta)):
        scalars_ref[i : i + 1, :] = jnp.broadcast_to(value, (1, 128))

    others(own_p, PLANE, lambda j: ask_copy(j, own_p).wait_send())
    others(col, n_cols, lambda j: item_copy(j, col).wait_send())
    others(col, n_cols, lambda j: user_copy(j, col).wait_send())
    others(own_a, GROUP, lambda j: gram_first(j, own_a).wait_send())
    others(own_b, GROUP, lambda j: gram_second(j, own_b).wait_send())
    others(own_a, GROUP, lambda j: gram_third(j, own_a).wait_send())
    for piece in range(PIECES):
        for step in range(last_step + 1):
            for way in range(2):
                for h in range(CHUNKS):
                    if z_travels(step, way, h):
                        z_copy(piece, way, step, h).wait_send()
        for half in range(2):
            others(own_p, PLANE, lambda j: plane_copy(piece, half, j, own_p).wait_send())
        for kind, owner, peer in ((0, col, right), (1, col, right), (2, col, left), (3, col, left), (4, left, right), (5, right, left)):
            x_copy(piece, kind, owner, peer).wait_send()
    others(own_a, GROUP, lambda j: sums_copy(0, peer_a, j, own_a).wait_send())
    others(own_b, GROUP, lambda j: sums_copy(1, peer_b, j, own_b).wait_send())
    for index in range(3):
        others(col, n_cols, lambda j: out_copy(index, j, col).wait_send())


def on_device(user_factors, item_factors, tile_user, tile_item, tile_count, tile_mask):
    n_cols = lax.axis_size("cols")
    col_width, users = user_factors.shape
    slots, tile_rows, tile_cols = tile_mask.shape
    width = col_width * n_cols
    blocks = users // tile_rows
    item_blocks = item_factors.shape[1] // tile_rows
    own_users = tile_rows // n_cols
    mine = blocks * own_users
    item_quarter = item_factors.shape[1] // n_cols
    vmem = pl.BlockSpec(memory_space=pltpu.VMEM)
    hbm = pl.BlockSpec(memory_space=pl.ANY)
    piece = width // GROUP
    dma = pltpu.SemaphoreType.DMA
    vectors, scalars = pl.pallas_call(
        kernel,
        out_shape=(
            jax.ShapeDtypeStruct((3, col_width, users), F32),
            jax.ShapeDtypeStruct((8, 128), F32),
        ),
        in_specs=[hbm] * 6,
        out_specs=(vmem, vmem),
        scratch_shapes=[
            pltpu.SMEM(tile_count.shape, jnp.int32),
            pltpu.SMEM(tile_user.shape, jnp.int32),
            pltpu.SMEM(tile_item.shape, jnp.int32),
            pltpu.VMEM((col_width, users), F32),
            pltpu.VMEM((col_width, item_factors.shape[1]), BF16),
            pltpu.VMEM((128, 128), jnp.int32),
            pltpu.VMEM((128, 128), jnp.int32),
            pltpu.VMEM((8, 128), jnp.int32),
            pltpu.SMEM((8, 128), jnp.int32),
            pltpu.VMEM((1, 128), jnp.int32),
            pltpu.VMEM((PLANE, 1, 128), jnp.int32),
            pltpu.VMEM((PLANE, 128), jnp.int32),
            pltpu.SMEM((PLANE, 128), jnp.int32),
            *[pltpu.VMEM((Z_CHIPS - 1, item_blocks, 16, 128), BF16)] * PIECES,
            *[pltpu.VMEM((item_blocks, 16, 128), BF16)] * PIECES,
            pltpu.VMEM((PIECES, PLANE, SLOTS, 16, 128), BF16),
            *[pltpu.VMEM((PLANE, SLOTS, 16, 128), BF16)] * PIECES,
            pltpu.VMEM((2, slots, width, 128), BF16),
            pltpu.VMEM((slots, own_users, tile_cols), BF16),
            pltpu.VMEM((n_cols, col_width, mine), F32),
            pltpu.VMEM((width, mine), F32),
            pltpu.VMEM((width, item_quarter), BF16),
            pltpu.VMEM((GROUP, piece, width), F32),
            pltpu.VMEM((GROUP, piece, width), F32),
            pltpu.VMEM((piece, width), F32),
            pltpu.VMEM((GROUP, piece, width), F32),
            pltpu.VMEM((GROUP, piece, width), F32),
            pltpu.VMEM((2, 1, 128), F32),
            pltpu.VMEM((2, GROUP, 1, 128), F32),
            pltpu.VMEM((blocks, 2 * own_users, width), BF16),
            pltpu.VMEM((slots, own_users, width), F32),
            pltpu.VMEM((mine, width), F32),
            pltpu.VMEM((mine, width), F32),
            pltpu.VMEM((mine, width), F32),
            pltpu.VMEM((mine, width), F32),
            pltpu.VMEM((3, n_cols, col_width, mine), F32),
            pltpu.VMEM((3, n_cols, col_width, mine), F32),
            dma((3,)),
            dma,
            dma,
            dma,
            dma,
            dma,
            dma((PLANE,)),
            dma((PLANE,)),
            dma((PIECES, 2, Z_CHIPS // 2, CHUNKS)),
            dma((PIECES, 2, Z_CHIPS // 2, CHUNKS)),
            dma((PIECES, 2, PLANE)),
            dma((PIECES, 2, PLANE)),
            dma((PIECES, 6)),
            dma((PIECES, 6)),
            dma((n_cols,)),
            dma((n_cols,)),
            dma((n_cols,)),
            dma((n_cols,)),
            dma((3, GROUP)),
            dma((3, GROUP)),
            dma((2, GROUP)),
            dma((2, GROUP)),
            dma((3, n_cols)),
            dma((3, n_cols)),
        ],
        compiler_params=pltpu.CompilerParams(
            collective_id=0, has_side_effects=True, vmem_limit_bytes=VMEM_BYTES
        ),
    )(tile_count, tile_user, tile_item, user_factors, item_factors, tile_mask)
    start_r, image_r, image_w = vectors[0], vectors[1], vectors[2]
    theta, delta, alpha_0, alpha_1, beta = [scalars[i, 0] for i in range(5)]
    more = 1.0 + delta
    mid_r = more * (start_r - theta * image_r) - delta * start_r
    solution_field = user_factors + alpha_0 * start_r + alpha_1 * (mid_r + beta * start_r)
    residual = mid_r - alpha_1 * (more * image_w + (beta - delta) * image_r)
    return solution_field, residual


def solution(mesh):
    return jax.shard_map(
        on_device,
        mesh=mesh,
        in_specs=(
            P("cols", "rows"),
            P("cols", "rows"),
            P("rows"),
            P("rows"),
            P("rows"),
            P("rows", None, None),
        ),
        out_specs=(P("cols", "rows"), P("cols", "rows")),
        check_vma=False,
    )
```

```python
import functools

import jax
import jax.numpy as jnp
from jax import lax
from jax.experimental import pallas as pl
from jax.experimental.pallas import tpu as pltpu
from jax.sharding import PartitionSpec as P

RIDGE = 0.5
CONFIDENCE = 40.0
HIGHEST = lax.Precision.HIGHEST
MESH = pl.DeviceIdType.MESH
F32 = jnp.float32
BF16 = jnp.bfloat16
Y_CHIPS = 4
Z_CHIPS = 8
CORES = 2
GROUP = 16
PLANE = Y_CHIPS * CORES
CAPACITY = 2
SLOTS = Z_CHIPS * CAPACITY
PIECES = 4
CHUNKS = 4
NEAR = SLOTS - CAPACITY
UNROLL = 24
VMEM_BYTES = 56 * 1024 * 1024
STARTS = (0, 2, 4, 6)
PACK_AFTER = -0.5
PASS_AFTER = 0.5


def interleave(first, second, odd):
    low = lax.broadcasted_iota(jnp.int32, first.shape, 1) < 64
    if odd:
        return jnp.where(low, pltpu.roll(first, 64, 1), second)
    return jnp.where(low, first, pltpu.roll(second, 64, 1))


def kernel(
    count_hbm, user_hbm, item_hbm, users_in, items_in, mask_ref,
    solution_ref, residual_ref,
    count_ref, user_in, item_in, users_ref, items_ref, user_col, item_col, table, table_smem, ask, asked, asked_rows, asked_smem, ring_0, ring_1, ring_2, ring_3, far_0, far_1, far_2, far_3, plane_send,
    plane_recv_0, plane_recv_1, plane_recv_2, plane_recv_3, tiles, masks,
    users_send, users_recv, items_recv, gram_part, gram_recv, gram_piece, gram_all, gram,
    sums_send, sums_recv, halves, terms, state_x, state_r, state_d, image, out_send, out_recv,
    lists_sem, users_sem, items_sem, mask_sem, smem_sem, table_sem, a_send, a_recv, z_send, z_recv, y_send, y_recv, x_send, x_recv,
    u_send, u_recv, i_send, i_recv, g_send, g_recv, s_send, s_recv, o_send, o_recv,
):
    rings = (ring_0, ring_1, ring_2, ring_3)
    fars = (far_0, far_1, far_2, far_3)
    plane_recvs = (plane_recv_0, plane_recv_1, plane_recv_2, plane_recv_3)
    row = lax.axis_index("rows")
    col = lax.axis_index("cols")
    n_cols = lax.axis_size("cols")
    core = lax.rem(row, CORES)
    own_z = lax.rem(lax.div(row, CORES), Z_CHIPS)
    own_y = lax.div(row, GROUP)
    own_a = lax.rem(row, GROUP)
    own_b = col * Y_CHIPS + own_y
    own_p = own_y * CORES + core
    tile_total, own_users, _ = masks.shape
    col_width = users_ref.shape[0]
    blocks = halves.shape[0]
    item_blocks = ring_0.shape[1]
    item_quarter = items_recv.shape[1]
    part = item_blocks // CHUNKS

    def peer_a(j):
        return (own_y * GROUP + j, col)

    def peer_b(j):
        return (lax.rem(j, Y_CHIPS) * GROUP + own_a, lax.div(j, Y_CHIPS))

    def peer_p(j):
        return (lax.div(j, CORES) * GROUP + own_z * CORES + lax.rem(j, CORES), col)

    def peer_c(j):
        return (row, j)

    z_peers = [
        (own_y * GROUP + lax.rem(own_z + step, Z_CHIPS) * CORES + core, col) for step in (1, Z_CHIPS - 1)
    ]

    right, left = lax.rem(col + 1, n_cols), lax.rem(col + n_cols - 1, n_cols)
    across = lax.rem(col + 2, n_cols)
    half_slots = tile_total // 2

    def others(own, count, body):
        def step(i, carry):
            body(lax.rem(own + i, count))
            return carry

        lax.fori_loop(1, count, step, 0)

    def remote(src, dst, send_sem, recv_sem, peer):
        return pltpu.make_async_remote_copy(
            src_ref=src, dst_ref=dst, send_sem=send_sem, recv_sem=recv_sem, device_id=peer, device_id_type=MESH
        )

    items_copy = pltpu.make_async_copy(items_in, items_ref, items_sem)
    users_copy = pltpu.make_async_copy(users_in, users_ref, users_sem)
    items_copy.start()
    users_copy.start()
    list_copies = [
        pltpu.make_async_copy(src, dst, lists_sem.at[i])
        for i, (src, dst) in enumerate(((count_hbm, count_ref), (user_hbm, user_in), (item_hbm, item_in)))
    ]
    for copy in list_copies:
        copy.start()
    mask_copy = pltpu.make_async_copy(
        mask_ref.at[:, pl.ds(pl.multiple_of(col * own_users, own_users), own_users), :], masks, mask_sem
    )

    barrier = pltpu.get_barrier_semaphore()

    def greet(peer):
        pl.semaphore_signal(barrier, inc=1, device_id=peer, device_id_type=MESH)

    for peer in z_peers:
        greet(peer)
    others(own_p, PLANE, lambda j: greet(peer_p(j)))
    others(col, n_cols, lambda j: greet(peer_c(j)))

    def split_items(b, carry):
        block = items_ref[:, pl.ds(pl.multiple_of(b * 256, 256), 256)]
        for piece in range(PIECES):
            lane, sub = piece // 2, piece % 2
            rings[piece][0, b] = block[16 * sub : 16 * sub + 16, 128 * lane : 128 * lane + 128]
        return carry

    items_copy.wait()
    lax.fori_loop(0, item_blocks, split_items, 0, unroll=4)
    def make_tables():
        user_col[...] = jnp.zeros_like(user_col)
        item_col[...] = jnp.zeros_like(item_col)

        def fill(t, carry):
            user_col[pl.ds(t, 1), :] = jnp.full((1, 128), user_in[t], jnp.int32)
            item_col[pl.ds(t, 1), :] = jnp.full((1, 128), item_in[t], jnp.int32)
            return carry

        lax.fori_loop(0, tile_total, fill, 0, unroll=8)
        square = user_col.shape
        down = lax.broadcasted_iota(jnp.int32, square, 0)
        over = lax.broadcasted_iota(jnp.int32, square, 1)
        count = count_ref[0]
        live = down < count
        users_down, items_down = user_col[...], item_col[...]

        def total(cond, value, axis):
            return jnp.sum(jnp.where(cond, value, 0), axis=axis, keepdims=True)

        key = jnp.where(live, users_down, blocks) * 128 + down
        place = total(key.T < key, 1, 1)
        chosen = place == over
        holder = items_down // item_blocks
        earlier = (holder.T == holder) & (over < down) & (over < count)
        rank = jnp.minimum(total(earlier, 1, 1), CAPACITY - 1)
        peer = holder // GROUP * CORES + holder % CORES
        distance = (holder // CORES % Z_CHIPS - own_z + Z_CHIPS) % Z_CHIPS
        far = Z_CHIPS // 2
        distance = jnp.where(distance == far, Z_CHIPS - 1, jnp.where(distance > far, distance - 1, distance))
        raw = jnp.where(live, peer * SLOTS + distance * CAPACITY + rank, 0)
        ask[...] = total((raw == over) & live, items_down % item_blocks, 0)
        user = total(chosen, users_down, 0)
        up_to = total(live & (users_down <= over), 1, 0)
        lane = over[:1]
        rows = [
            total(chosen, raw, 0),
            total(chosen, down, 0),
            user,
            jnp.where((user == pltpu.roll(user, 1, 1)) & (lane > 0), 1, 0),
            jnp.where(lane < count, 1, 0),
            jnp.maximum(up_to - 1, 0),
            total(live & (users_down == over), 1, 0),
            jnp.zeros_like(user),
        ]
        table[...] = jnp.concatenate(rows, axis=0)
        pltpu.make_async_copy(table, table_smem, table_sem).start()

    for copy in list_copies:
        copy.wait()
    make_tables()
    users_copy.wait()
    for dest in range(n_cols):
        for pair in range(blocks // 2):
            at = (dest // 2) * 128
            first = users_ref[:, pl.ds(2 * pair * 256 + at, 128)]
            second = users_ref[:, pl.ds((2 * pair + 1) * 256 + at, 128)]
            users_send[dest, :, pl.ds(pair * 128, 128)] = interleave(first, second, dest % 2 == 1)
    pl.semaphore_wait(barrier, 2 + PLANE - 1 + n_cols - 1)

    def z_copy(piece, way, step, h):
        chunk = pl.ds(part * h, part)
        if way == 0:
            src = (Z_CHIPS - 1 - step) % (Z_CHIPS - 1)
            dst = Z_CHIPS - 2 - step
        else:
            src, dst = step, step + 1
        target = rings[piece].at[dst, chunk] if step < last_step else fars[piece].at[chunk]
        return remote(
            rings[piece].at[src, chunk], target,
            z_send.at[piece, way, step, h], z_recv.at[piece, way, step, h], z_peers[way],
        )

    last_step = Z_CHIPS // 2 - 1

    def z_travels(step, way, h):
        return step < last_step or (h < CHUNKS // 2) == (way == 0)

    def z_step(piece, step):
        for h in range(CHUNKS):
            for way in range(2):
                if step > 0 and z_travels(step - 1, way, h):
                    z_copy(piece, way, step - 1, h).wait_recv()
                if step <= last_step and z_travels(step, way, h):
                    z_copy(piece, way, step, h).start()

    def ask_copy(j, slot):
        return remote(ask, asked.at[slot], a_send.at[j], a_recv.at[slot], peer_p(j))

    def plane_copy(piece, half, j, slot):
        first, count = ((0, NEAR), (NEAR, CAPACITY))[half]
        return remote(
            plane_send.at[piece, j, pl.ds(first, count)], plane_recvs[piece].at[slot, pl.ds(first, count)],
            y_send.at[piece, half, j], y_recv.at[piece, half, slot], peer_p(j),
        )

    def plane_begin(piece, half):
        first, count = ((0, NEAR), (NEAR, CAPACITY))[half]

        def pick(j, carry):
            for slot in range(first, first + count):
                if half == 0:
                    block = rings[piece][slot // CAPACITY, asked_smem[j, own_p * SLOTS + slot]]
                else:
                    block = fars[piece][asked_smem[j, own_p * SLOTS + slot]]
                plane_send[piece, j, slot] = block
            return carry

        lax.fori_loop(0, PLANE, pick, 0, unroll=2)
        others(own_p, PLANE, lambda j: plane_copy(piece, half, j, own_p).start())
        plane_recvs[piece][own_p, pl.ds(first, count)] = plane_send[piece, own_p, pl.ds(first, count)]

    def x_copy(piece, kind, owner, peer):
        half = (0, 1, 0, 1, 0, 1)[kind]
        rows_at = pl.multiple_of(owner * col_width + 16 * (piece % 2), 16)
        at = tiles.at[piece // 2, pl.ds(half * half_slots, half_slots), pl.ds(rows_at, 16), :]
        return remote(at, at, x_send.at[piece, kind], x_recv.at[piece, kind], (row, peer))

    def x_begin(piece):
        for half in range(2):
            others(own_p, PLANE, lambda j: plane_copy(piece, half, j, j).wait_recv())
        rows_at = pl.multiple_of(col * col_width + 16 * (piece % 2), 16)

        def pack(s, carry):
            raw = table_smem[0, s]
            tiles[piece // 2, s, pl.ds(rows_at, 16), :] = plane_recvs[piece][raw >> 4, raw & (SLOTS - 1)]
            return carry

        lax.fori_loop(0, tile_total, pack, 0, unroll=8)
        for kind, peer in ((0, right), (3, left), (1, right), (2, left)):
            x_copy(piece, kind, col, peer).start()

    def x_forward(piece):
        x_copy(piece, 0, left, right).wait_recv()
        x_copy(piece, 4, left, right).start()
        x_copy(piece, 3, right, left).wait_recv()
        x_copy(piece, 5, right, left).start()

    def x_end(piece):
        x_copy(piece, 1, left, right).wait_recv()
        x_copy(piece, 2, right, left).wait_recv()
        x_copy(piece, 4, across, left).wait_recv()
        x_copy(piece, 5, across, left).wait_recv()

    own_cols = pl.ds(pl.multiple_of(col * col_width, col_width), col_width)

    def item_quarter_ref(j):
        return items_ref.at[:, pl.ds(pl.multiple_of(j * item_quarter, item_quarter), item_quarter)]

    def col_rows(j):
        return pl.ds(pl.multiple_of(j * col_width, col_width), col_width)

    def item_copy(j, slot):
        return remote(item_quarter_ref(j), items_recv.at[col_rows(slot)], i_send.at[j], i_recv.at[slot], peer_c(j))

    def user_copy(j, slot):
        return remote(users_send.at[j], users_recv.at[col_rows(slot)], u_send.at[j], u_recv.at[slot], peer_c(j))

    def gram_first(j, slot):
        return remote(gram_part.at[j], gram_recv.at[slot], g_send.at[0, j], g_recv.at[0, slot], peer_a(j))

    def gram_second(j, slot):
        return remote(gram_piece, gram_all.at[slot], g_send.at[1, j], g_recv.at[1, slot], peer_b(j))

    def gram_third(j, slot):
        return remote(gram.at[own_a], gram.at[slot], g_send.at[2, j], g_recv.at[2, slot], peer_a(j))

    def gram_1():
        others(col, n_cols, lambda j: item_copy(j, j).wait_recv())
        table = items_recv[...]
        gram_part[...] = lax.dot_general(
            table, table, (((1,), (1,)), ((), ())), preferred_element_type=F32
        ).reshape(gram_part.shape)
        others(own_a, GROUP, lambda j: gram_first(j, own_a).start())
        gram_recv[own_a] = gram_part[own_a]

    def gram_2():
        others(own_a, GROUP, lambda j: gram_first(j, j).wait_recv())
        gram_piece[...] = jnp.sum(gram_recv[...], axis=0)
        others(own_b, GROUP, lambda j: gram_second(j, own_b).start())
        gram_all[own_b] = gram_piece[...]

    def gram_3():
        others(own_b, GROUP, lambda j: gram_second(j, j).wait_recv())
        gram[own_a] = jnp.sum(gram_all[...], axis=0)
        others(own_a, GROUP, lambda j: gram_third(j, own_a).start())

    def sparse_part(vectors, lanes, first_time):
        high = vectors.astype(BF16)
        low = (vectors - high.astype(F32)).astype(BF16)
        halves[:, :own_users] = high.reshape(blocks, own_users, 128)
        halves[:, own_users:] = low.reshape(blocks, own_users, 128)

        def step(s, running):
            if len(lanes) == 2:
                item = jnp.concatenate([tiles[0, s], tiles[1, s]], axis=1)
                mask = masks[table_smem[1, s]]
            else:
                item = tiles[lanes[0], s]
                mask = masks[table_smem[1, s], :, pl.ds(128 * lanes[0], 128)]
            mask = mask.astype(F32) * table_smem[4, s].astype(F32)
            scores = jnp.dot(halves[table_smem[2, s]], item, preferred_element_type=F32)
            scores = scores[:own_users] + scores[own_users:]
            if first_time:
                strengths = mask * ((1.0 + CONFIDENCE) - CONFIDENCE * scores)
            else:
                strengths = mask * scores
            s_high = strengths.astype(BF16)
            s_low = (strengths - s_high.astype(F32)).astype(BF16)
            both = lax.dot_general(
                jnp.concatenate([s_high, s_low], axis=0), item, (((1,), (1,)), ((), ())),
                preferred_element_type=F32,
            )
            running = both[:own_users] + both[own_users:] + table_smem[3, s].astype(F32) * running
            terms[s] = running
            return running

        lax.fori_loop(0, tile_total, step, jnp.zeros((own_users, 128), F32), unroll=UNROLL)
        return jnp.concatenate([jnp.where(table_smem[6, b] > 0, terms[table_smem[5, b]], 0.0) for b in range(blocks)], axis=0)

    def dense_part(vectors):
        return (
            jnp.dot(vectors, gram[...].reshape(128, 128), precision=HIGHEST, preferred_element_type=F32)
            + RIDGE * vectors
        )

    def sums_copy(at, peer, j, slot):
        return remote(sums_send.at[at], sums_recv.at[at, slot], s_send.at[at, j], s_recv.at[at, slot], peer(j))

    def all_sums(products, meanwhile):
        rows = [jnp.sum(p, axis=0, keepdims=True) for p in products]
        rows.append(jnp.zeros((8 - len(rows), 128), F32))
        total = jnp.sum(jnp.concatenate(rows, axis=0), axis=1, keepdims=True)
        at_lane = lax.broadcasted_iota(jnp.int32, (8, 128), 0) == lax.broadcasted_iota(jnp.int32, (8, 128), 1)
        total = jnp.sum(jnp.where(at_lane, total, 0.0), axis=0, keepdims=True)
        for at, (peer, own) in enumerate(((peer_a, own_a), (peer_b, own_b))):
            sums_send[at] = total
            others(own, GROUP, lambda j: sums_copy(at, peer, j, own).start())
            sums_recv[at, own] = total
            if at == 0:
                meanwhile()
            others(own, GROUP, lambda j: sums_copy(at, peer, j, j).wait_recv())
            total = jnp.sum(sums_recv[at], axis=0)
        return [total[:, i : i + 1] for i in range(len(products))]

    def out_copy(index, j, slot):
        return remote(
            out_send.at[index, j], out_recv.at[index, slot], o_send.at[index, j], o_recv.at[index, slot], peer_c(j)
        )

    def out_begin(index, vectors):
        out_send[index] = vectors.T.reshape(n_cols, col_width, blocks * own_users)
        others(col, n_cols, lambda j: out_copy(index, j, col).start())
        out_recv[index, col] = out_send[index, col]

    def out_end(index):
        others(col, n_cols, lambda j: out_copy(index, j, j).wait_recv())

    z_step(0, 0)
    mask_copy.start()
    others(own_p, PLANE, lambda j: ask_copy(j, own_p).start())
    asked[own_p] = ask[...]
    others(col, n_cols, lambda j: item_copy(j, col).start())
    z_step(0, 1)
    others(col, n_cols, lambda j: user_copy(j, col).start())
    items_recv[own_cols, :] = item_quarter_ref(col)[...]
    users_recv[own_cols, :] = users_send[col]

    def asked_ready():
        others(own_p, PLANE, lambda j: ask_copy(j, j).wait_recv())
        asked_rows[...] = asked[:, 0, :]
        to_smem = pltpu.make_async_copy(asked_rows, asked_smem, smem_sem)
        to_smem.start()
        to_smem.wait()
        pltpu.make_async_copy(table, table_smem, table_sem).wait()

    span = last_step + 2
    def first_half():
        others(col, n_cols, lambda j: user_copy(j, j).wait_recv())
        state_x[...] = users_recv[...].T
        mask_copy.wait()
        x_end(1)
        state_r[...] = sparse_part(state_x[...], (0,), True)

    def gram_middle():
        x_end(0)
        gram_2()

    events = []
    for piece, start in enumerate(STARTS):
        for step in range(span):
            if (piece, step) not in ((0, 0), (0, 1)):
                events.append((start + step, functools.partial(z_step, piece, step)))
            if step == span - 2:
                if piece == 0:
                    events.append((start + step, asked_ready))
                events.append((start + step, functools.partial(plane_begin, piece, 0)))
            if step == span - 1:
                events.append((start + step, functools.partial(plane_begin, piece, 1)))
        events.append((start + span + PACK_AFTER, functools.partial(x_begin, piece)))
        events.append((start + span + PASS_AFTER, functools.partial(x_forward, piece)))
    events.append((STARTS[0] + span, gram_1))
    events.append((STARTS[0] + span + 2, gram_middle))
    events.append((STARTS[0] + span + 4, gram_3))
    events.append((STARTS[-1] + span, first_half))
    for _, event in sorted(events, key=lambda item: item[0]):
        event()
    others(own_a, GROUP, lambda j: gram_third(j, j).wait_recv())
    state_r[...] -= dense_part(state_x[...])
    x_end(2)
    x_end(3)

    state_r[...] += sparse_part(state_x[...], (1,), True)
    out_begin(0, state_r[...])
    image[...] = dense_part(state_r[...]) + CONFIDENCE * sparse_part(state_r[...], (0, 1), False)

    full = gram[...].reshape(128, 128)
    diagonal = lax.broadcasted_iota(jnp.int32, full.shape, 0) == lax.broadcasted_iota(jnp.int32, full.shape, 1)
    trace = jnp.sum(jnp.sum(jnp.where(diagonal, full, 0.0), axis=0, keepdims=True), axis=1, keepdims=True)
    theta = 1.0 / (trace * (1.0 / 128) + RIDGE)
    state_d[...] = state_r[...] - theta * image[...]
    image_w = dense_part(state_d[...]) + CONFIDENCE * sparse_part(state_d[...], (0, 1), False)

    def images_out():
        out_begin(2, image_w)
        out_begin(1, image[...])

    rr, rw, ww, ri, wi, rj, wj = all_sums(
        [
            state_r[...] * state_r[...],
            state_r[...] * state_d[...],
            state_d[...] * state_d[...],
            state_r[...] * image[...],
            state_d[...] * image[...],
            state_r[...] * image_w,
            state_d[...] * image_w,
        ],
        images_out,
    )
    delta = rw / (rr - rw)
    more = 1.0 + delta
    alpha_0 = theta * more
    norm_1 = delta * delta * rr - 2.0 * delta * more * rw + more * more * ww
    beta = norm_1 / rr
    curve_1 = (
        more * more * wj
        - delta * more * (wi + rj)
        + delta * delta * ri
        + beta * (more * (wi + rj) - 2.0 * delta * ri)
        + beta * beta * ri
    )
    alpha_1 = norm_1 / curve_1

    for index in range(3):
        out_end(index)
    for block in range(blocks):
        lanes = pl.ds((block // 2) * 128, 128)
        for side in range(n_cols // 2):
            start_r, image_r, image_d = [
                interleave(out_recv[i, 2 * side, :, lanes], out_recv[i, 2 * side + 1, :, lanes], block % 2 == 1)
                for i in range(3)
            ]
            here = pl.ds(block * 256 + side * 128, 128)
            mid_r = more * (start_r - theta * image_r) - delta * start_r
            mid_x = users_ref[:, here] + alpha_0 * start_r
            solution_ref[:, here] = mid_x + alpha_1 * (mid_r + beta * start_r)
            residual_ref[:, here] = mid_r - alpha_1 * (more * image_d + (beta - delta) * image_r)

    others(own_p, PLANE, lambda j: ask_copy(j, own_p).wait_send())
    others(col, n_cols, lambda j: item_copy(j, col).wait_send())
    others(col, n_cols, lambda j: user_copy(j, col).wait_send())
    others(own_a, GROUP, lambda j: gram_first(j, own_a).wait_send())
    others(own_b, GROUP, lambda j: gram_second(j, own_b).wait_send())
    others(own_a, GROUP, lambda j: gram_third(j, own_a).wait_send())
    for piece in range(PIECES):
        for step in range(last_step + 1):
            for way in range(2):
                for h in range(CHUNKS):
                    if z_travels(step, way, h):
                        z_copy(piece, way, step, h).wait_send()
        for half in range(2):
            others(own_p, PLANE, lambda j: plane_copy(piece, half, j, own_p).wait_send())
        for kind, owner, peer in ((0, col, right), (1, col, right), (2, col, left), (3, col, left), (4, left, right), (5, right, left)):
            x_copy(piece, kind, owner, peer).wait_send()
    others(own_a, GROUP, lambda j: sums_copy(0, peer_a, j, own_a).wait_send())
    others(own_b, GROUP, lambda j: sums_copy(1, peer_b, j, own_b).wait_send())
    for index in range(3):
        others(col, n_cols, lambda j: out_copy(index, j, col).wait_send())


def on_device(user_factors, item_factors, tile_user, tile_item, tile_count, tile_mask):
    n_cols = lax.axis_size("cols")
    col_width, users = user_factors.shape
    slots, tile_rows, tile_cols = tile_mask.shape
    width = col_width * n_cols
    blocks = users // tile_rows
    item_blocks = item_factors.shape[1] // tile_rows
    own_users = tile_rows // n_cols
    mine = blocks * own_users
    item_quarter = item_factors.shape[1] // n_cols
    vmem = pl.BlockSpec(memory_space=pltpu.VMEM)
    hbm = pl.BlockSpec(memory_space=pl.ANY)
    piece = width // GROUP
    dma = pltpu.SemaphoreType.DMA
    out = jax.ShapeDtypeStruct((col_width, users), F32)
    return pl.pallas_call(
        kernel,
        out_shape=(out, out),
        in_specs=[hbm] * 6,
        out_specs=(vmem, vmem),
        scratch_shapes=[
            pltpu.SMEM(tile_count.shape, jnp.int32),
            pltpu.SMEM(tile_user.shape, jnp.int32),
            pltpu.SMEM(tile_item.shape, jnp.int32),
            pltpu.VMEM((col_width, users), F32),
            pltpu.VMEM((col_width, item_factors.shape[1]), BF16),
            pltpu.VMEM((128, 128), jnp.int32),
            pltpu.VMEM((128, 128), jnp.int32),
            pltpu.VMEM((8, 128), jnp.int32),
            pltpu.SMEM((8, 128), jnp.int32),
            pltpu.VMEM((1, 128), jnp.int32),
            pltpu.VMEM((PLANE, 1, 128), jnp.int32),
            pltpu.VMEM((PLANE, 128), jnp.int32),
            pltpu.SMEM((PLANE, 128), jnp.int32),
            *[pltpu.VMEM((Z_CHIPS - 1, item_blocks, 16, 128), BF16)] * PIECES,
            *[pltpu.VMEM((item_blocks, 16, 128), BF16)] * PIECES,
            pltpu.VMEM((PIECES, PLANE, SLOTS, 16, 128), BF16),
            *[pltpu.VMEM((PLANE, SLOTS, 16, 128), BF16)] * PIECES,
            pltpu.VMEM((2, slots, width, 128), BF16),
            pltpu.VMEM((slots, own_users, tile_cols), BF16),
            pltpu.VMEM((n_cols, col_width, mine), F32),
            pltpu.VMEM((width, mine), F32),
            pltpu.VMEM((width, item_quarter), BF16),
            pltpu.VMEM((GROUP, piece, width), F32),
            pltpu.VMEM((GROUP, piece, width), F32),
            pltpu.VMEM((piece, width), F32),
            pltpu.VMEM((GROUP, piece, width), F32),
            pltpu.VMEM((GROUP, piece, width), F32),
            pltpu.VMEM((2, 1, 128), F32),
            pltpu.VMEM((2, GROUP, 1, 128), F32),
            pltpu.VMEM((blocks, 2 * own_users, width), BF16),
            pltpu.VMEM((slots, own_users, width), F32),
            pltpu.VMEM((mine, width), F32),
            pltpu.VMEM((mine, width), F32),
            pltpu.VMEM((mine, width), F32),
            pltpu.VMEM((mine, width), F32),
            pltpu.VMEM((3, n_cols, col_width, mine), F32),
            pltpu.VMEM((3, n_cols, col_width, mine), F32),
            dma((3,)),
            dma,
            dma,
            dma,
            dma,
            dma,
            dma((PLANE,)),
            dma((PLANE,)),
            dma((PIECES, 2, Z_CHIPS // 2, CHUNKS)),
            dma((PIECES, 2, Z_CHIPS // 2, CHUNKS)),
            dma((PIECES, 2, PLANE)),
            dma((PIECES, 2, PLANE)),
            dma((PIECES, 6)),
            dma((PIECES, 6)),
            dma((n_cols,)),
            dma((n_cols,)),
            dma((n_cols,)),
            dma((n_cols,)),
            dma((3, GROUP)),
            dma((3, GROUP)),
            dma((2, GROUP)),
            dma((2, GROUP)),
            dma((3, n_cols)),
            dma((3, n_cols)),
        ],
        compiler_params=pltpu.CompilerParams(
            collective_id=0, has_side_effects=True, vmem_limit_bytes=VMEM_BYTES
        ),
    )(tile_count, tile_user, tile_item, user_factors, item_factors, tile_mask)


def solution(mesh):
    return jax.shard_map(
        on_device,
        mesh=mesh,
        in_specs=(
            P("cols", "rows"),
            P("cols", "rows"),
            P("rows"),
            P("rows"),
            P("rows"),
            P("rows", None, None),
        ),
        out_specs=(P("cols", "rows"), P("cols", "rows")),
        check_vma=False,
    )
```

```python
import functools

import jax
import jax.numpy as jnp
from jax import lax
from jax.experimental import pallas as pl
from jax.experimental.pallas import tpu as pltpu
from jax.sharding import PartitionSpec as P

RIDGE = 0.5
CONFIDENCE = 40.0
HIGHEST = lax.Precision.HIGHEST
MESH = pl.DeviceIdType.MESH
F32 = jnp.float32
BF16 = jnp.bfloat16
Y_CHIPS = 4
Z_CHIPS = 8
CORES = 2
GROUP = 16
PLANE = Y_CHIPS * CORES
CAPACITY = 2
SLOTS = Z_CHIPS * CAPACITY
PIECES = 4
CHUNKS = 4
NEAR = SLOTS - CAPACITY
UNROLL = 24
VMEM_BYTES = 56 * 1024 * 1024
STARTS = (0, 2, 4, 6)
PACK_AFTER = -0.5
PASS_AFTER = 0.5


def interleave(first, second, odd):
    low = lax.broadcasted_iota(jnp.int32, first.shape, 1) < 64
    if odd:
        return jnp.where(low, pltpu.roll(first, 64, 1), second)
    return jnp.where(low, first, pltpu.roll(second, 64, 1))


def kernel(
    count_hbm, user_hbm, item_hbm, users_in, items_in, mask_ref,
    solution_ref, residual_ref,
    count_ref, user_in, item_in, users_ref, items_ref, user_col, item_col, table, table_smem, ask, asked, asked_rows, asked_smem, ring_0, ring_1, ring_2, ring_3, far_0, far_1, far_2, far_3, plane_send,
    plane_recv_0, plane_recv_1, plane_recv_2, plane_recv_3, tiles, masks,
    users_send, users_recv, items_recv, gram_part, gram_recv, gram_piece, gram_all, gram,
    sums_send, sums_recv, halves, terms, state_x, state_r, state_d, image, out_send, out_recv,
    lists_sem, users_sem, items_sem, mask_sem, smem_sem, table_sem, a_send, a_recv, z_send, z_recv, y_send, y_recv, x_send, x_recv,
    u_send, u_recv, i_send, i_recv, g_send, g_recv, s_send, s_recv, o_send, o_recv,
):
    rings = (ring_0, ring_1, ring_2, ring_3)
    fars = (far_0, far_1, far_2, far_3)
    plane_recvs = (plane_recv_0, plane_recv_1, plane_recv_2, plane_recv_3)
    row = lax.axis_index("rows")
    col = lax.axis_index("cols")
    n_cols = lax.axis_size("cols")
    core = lax.rem(row, CORES)
    own_z = lax.rem(lax.div(row, CORES), Z_CHIPS)
    own_y = lax.div(row, GROUP)
    own_a = lax.rem(row, GROUP)
    own_b = col * Y_CHIPS + own_y
    own_p = own_y * CORES + core
    tile_total, own_users, _ = masks.shape
    col_width = users_ref.shape[0]
    blocks = halves.shape[0]
    item_blocks = ring_0.shape[1]
    item_quarter = items_recv.shape[1]
    part = item_blocks // CHUNKS

    def peer_a(j):
        return (own_y * GROUP + j, col)

    def peer_b(j):
        return (lax.rem(j, Y_CHIPS) * GROUP + own_a, lax.div(j, Y_CHIPS))

    def peer_p(j):
        return (lax.div(j, CORES) * GROUP + own_z * CORES + lax.rem(j, CORES), col)

    def peer_c(j):
        return (row, j)

    z_peers = [
        (own_y * GROUP + lax.rem(own_z + step, Z_CHIPS) * CORES + core, col) for step in (1, Z_CHIPS - 1)
    ]

    right, left = lax.rem(col + 1, n_cols), lax.rem(col + n_cols - 1, n_cols)
    across = lax.rem(col + 2, n_cols)
    half_slots = tile_total // 2

    def others(own, count, body):
        def step(i, carry):
            body(lax.rem(own + i, count))
            return carry

        lax.fori_loop(1, count, step, 0)

    def remote(src, dst, send_sem, recv_sem, peer):
        return pltpu.make_async_remote_copy(
            src_ref=src, dst_ref=dst, send_sem=send_sem, recv_sem=recv_sem, device_id=peer, device_id_type=MESH
        )

    items_copy = pltpu.make_async_copy(items_in, items_ref, items_sem)
    users_copy = pltpu.make_async_copy(users_in, users_ref, users_sem)
    items_copy.start()
    users_copy.start()
    list_copies = [
        pltpu.make_async_copy(src, dst, lists_sem.at[i])
        for i, (src, dst) in enumerate(((count_hbm, count_ref), (user_hbm, user_in), (item_hbm, item_in)))
    ]
    for copy in list_copies:
        copy.start()
    mask_copy = pltpu.make_async_copy(
        mask_ref.at[:, pl.ds(pl.multiple_of(col * own_users, own_users), own_users), :], masks, mask_sem
    )

    barrier = pltpu.get_barrier_semaphore()

    def greet(peer):
        pl.semaphore_signal(barrier, inc=1, device_id=peer, device_id_type=MESH)

    for peer in z_peers:
        greet(peer)
    others(own_p, PLANE, lambda j: greet(peer_p(j)))
    others(col, n_cols, lambda j: greet(peer_c(j)))

    def split_items(b, carry):
        block = items_ref[:, pl.ds(pl.multiple_of(b * 256, 256), 256)]
        for piece in range(PIECES):
            lane, sub = piece // 2, piece % 2
            rings[piece][0, b] = block[16 * sub : 16 * sub + 16, 128 * lane : 128 * lane + 128]
        return carry

    items_copy.wait()
    lax.fori_loop(0, item_blocks, split_items, 0, unroll=4)
    def make_tables():
        user_col[...] = jnp.zeros_like(user_col)
        item_col[...] = jnp.zeros_like(item_col)

        def fill(t, carry):
            user_col[pl.ds(t, 1), :] = jnp.full((1, 128), user_in[t], jnp.int32)
            item_col[pl.ds(t, 1), :] = jnp.full((1, 128), item_in[t], jnp.int32)
            return carry

        lax.fori_loop(0, tile_total, fill, 0, unroll=8)
        square = user_col.shape
        down = lax.broadcasted_iota(jnp.int32, square, 0)
        over = lax.broadcasted_iota(jnp.int32, square, 1)
        count = count_ref[0]
        live = down < count
        users_down, items_down = user_col[...], item_col[...]

        def total(cond, value, axis):
            return jnp.sum(jnp.where(cond, value, 0), axis=axis, keepdims=True)

        key = jnp.where(live, users_down, blocks) * 128 + down
        place = total(key.T < key, 1, 1)
        chosen = place == over
        holder = items_down // item_blocks
        earlier = (holder.T == holder) & (over < down) & (over < count)
        rank = jnp.minimum(total(earlier, 1, 1), CAPACITY - 1)
        peer = holder // GROUP * CORES + holder % CORES
        distance = (holder // CORES % Z_CHIPS - own_z + Z_CHIPS) % Z_CHIPS
        far = Z_CHIPS // 2
        distance = jnp.where(distance == far, Z_CHIPS - 1, jnp.where(distance > far, distance - 1, distance))
        raw = jnp.where(live, peer * SLOTS + distance * CAPACITY + rank, 0)
        ask[...] = total((raw == over) & live, items_down % item_blocks, 0)
        user = total(chosen, users_down, 0)
        up_to = total(live & (users_down <= over), 1, 0)
        lane = over[:1]
        rows = [
            total(chosen, raw, 0),
            total(chosen, down, 0),
            user,
            jnp.where((user == pltpu.roll(user, 1, 1)) & (lane > 0), 1, 0),
            jnp.where(lane < count, 1, 0),
            jnp.maximum(up_to - 1, 0),
            total(live & (users_down == over), 1, 0),
            jnp.zeros_like(user),
        ]
        table[...] = jnp.concatenate(rows, axis=0)
        pltpu.make_async_copy(table, table_smem, table_sem).start()

    for copy in list_copies:
        copy.wait()
    make_tables()
    users_copy.wait()
    for dest in range(n_cols):
        for pair in range(blocks // 2):
            at = (dest // 2) * 128
            first = users_ref[:, pl.ds(2 * pair * 256 + at, 128)]
            second = users_ref[:, pl.ds((2 * pair + 1) * 256 + at, 128)]
            users_send[dest, :, pl.ds(pair * 128, 128)] = interleave(first, second, dest % 2 == 1)
    pl.semaphore_wait(barrier, 2 + PLANE - 1 + n_cols - 1)

    def z_copy(piece, way, step, h):
        chunk = pl.ds(part * h, part)
        if way == 0:
            src = (Z_CHIPS - 1 - step) % (Z_CHIPS - 1)
            dst = Z_CHIPS - 2 - step
        else:
            src, dst = step, step + 1
        target = rings[piece].at[dst, chunk] if step < last_step else fars[piece].at[chunk]
        return remote(
            rings[piece].at[src, chunk], target,
            z_send.at[piece, way, step, h], z_recv.at[piece, way, step, h], z_peers[way],
        )

    last_step = Z_CHIPS // 2 - 1

    def z_travels(step, way, h):
        return step < last_step or (h < CHUNKS // 2) == (way == 0)

    def z_step(piece, step):
        for h in range(CHUNKS):
            for way in range(2):
                if step > 0 and z_travels(step - 1, way, h):
                    z_copy(piece, way, step - 1, h).wait_recv()
                if step <= last_step and z_travels(step, way, h):
                    z_copy(piece, way, step, h).start()

    def ask_copy(j, slot):
        return remote(ask, asked.at[slot], a_send.at[j], a_recv.at[slot], peer_p(j))

    def plane_copy(piece, half, j, slot):
        first, count = ((0, NEAR), (NEAR, CAPACITY))[half]
        return remote(
            plane_send.at[piece, j, pl.ds(first, count)], plane_recvs[piece].at[slot, pl.ds(first, count)],
            y_send.at[piece, half, j], y_recv.at[piece, half, slot], peer_p(j),
        )

    def plane_begin(piece, half):
        first, count = ((0, NEAR), (NEAR, CAPACITY))[half]

        def pick(j, carry):
            for slot in range(first, first + count):
                if half == 0:
                    block = rings[piece][slot // CAPACITY, asked_smem[j, own_p * SLOTS + slot]]
                else:
                    block = fars[piece][asked_smem[j, own_p * SLOTS + slot]]
                plane_send[piece, j, slot] = block
            return carry

        lax.fori_loop(0, PLANE, pick, 0, unroll=2)
        others(own_p, PLANE, lambda j: plane_copy(piece, half, j, own_p).start())
        plane_recvs[piece][own_p, pl.ds(first, count)] = plane_send[piece, own_p, pl.ds(first, count)]

    def x_copy(piece, kind, owner, peer):
        half = (0, 1, 0, 1, 0, 1)[kind]
        rows_at = pl.multiple_of(owner * col_width + 16 * (piece % 2), 16)
        at = tiles.at[piece // 2, pl.ds(half * half_slots, half_slots), pl.ds(rows_at, 16), :]
        return remote(at, at, x_send.at[piece, kind], x_recv.at[piece, kind], (row, peer))

    def x_begin(piece):
        for half in range(2):
            others(own_p, PLANE, lambda j: plane_copy(piece, half, j, j).wait_recv())
        rows_at = pl.multiple_of(col * col_width + 16 * (piece % 2), 16)

        def pack(s, carry):
            raw = table_smem[0, s]
            tiles[piece // 2, s, pl.ds(rows_at, 16), :] = plane_recvs[piece][raw >> 4, raw & (SLOTS - 1)]
            return carry

        lax.fori_loop(0, tile_total, pack, 0, unroll=8)
        for kind, peer in ((0, right), (3, left), (1, right), (2, left)):
            x_copy(piece, kind, col, peer).start()

    def x_forward(piece):
        x_copy(piece, 0, left, right).wait_recv()
        x_copy(piece, 4, left, right).start()
        x_copy(piece, 3, right, left).wait_recv()
        x_copy(piece, 5, right, left).start()

    def x_end(piece):
        x_copy(piece, 1, left, right).wait_recv()
        x_copy(piece, 2, right, left).wait_recv()
        x_copy(piece, 4, across, left).wait_recv()
        x_copy(piece, 5, across, left).wait_recv()

    own_cols = pl.ds(pl.multiple_of(col * col_width, col_width), col_width)

    def item_quarter_ref(j):
        return items_ref.at[:, pl.ds(pl.multiple_of(j * item_quarter, item_quarter), item_quarter)]

    def col_rows(j):
        return pl.ds(pl.multiple_of(j * col_width, col_width), col_width)

    def item_copy(j, slot):
        return remote(item_quarter_ref(j), items_recv.at[col_rows(slot)], i_send.at[j], i_recv.at[slot], peer_c(j))

    def user_copy(j, slot):
        return remote(users_send.at[j], users_recv.at[col_rows(slot)], u_send.at[j], u_recv.at[slot], peer_c(j))

    def gram_first(j, slot):
        return remote(gram_part.at[j], gram_recv.at[slot], g_send.at[0, j], g_recv.at[0, slot], peer_a(j))

    def gram_second(j, slot):
        return remote(gram_piece, gram_all.at[slot], g_send.at[1, j], g_recv.at[1, slot], peer_b(j))

    def gram_third(j, slot):
        return remote(gram.at[own_a], gram.at[slot], g_send.at[2, j], g_recv.at[2, slot], peer_a(j))

    def gram_1():
        others(col, n_cols, lambda j: item_copy(j, j).wait_recv())
        table = items_recv[...]
        gram_part[...] = lax.dot_general(
            table, table, (((1,), (1,)), ((), ())), preferred_element_type=F32
        ).reshape(gram_part.shape)
        others(own_a, GROUP, lambda j: gram_first(j, own_a).start())
        gram_recv[own_a] = gram_part[own_a]

    def gram_2():
        others(own_a, GROUP, lambda j: gram_first(j, j).wait_recv())
        gram_piece[...] = jnp.sum(gram_recv[...], axis=0)
        others(own_b, GROUP, lambda j: gram_second(j, own_b).start())
        gram_all[own_b] = gram_piece[...]

    def gram_3():
        others(own_b, GROUP, lambda j: gram_second(j, j).wait_recv())
        gram[own_a] = jnp.sum(gram_all[...], axis=0)
        others(own_a, GROUP, lambda j: gram_third(j, own_a).start())

    def sparse_part(vectors, lanes, first_time):
        high = vectors.astype(BF16)
        low = (vectors - high.astype(F32)).astype(BF16)
        halves[:, :own_users] = high.reshape(blocks, own_users, 128)
        halves[:, own_users:] = low.reshape(blocks, own_users, 128)

        def step(s, running):
            if len(lanes) == 2:
                item = jnp.concatenate([tiles[0, s], tiles[1, s]], axis=1)
                mask = masks[table_smem[1, s]]
            else:
                item = tiles[lanes[0], s]
                mask = masks[table_smem[1, s], :, pl.ds(128 * lanes[0], 128)]
            mask = mask.astype(F32) * table_smem[4, s].astype(F32)
            scores = jnp.dot(halves[table_smem[2, s]], item, preferred_element_type=F32)
            scores = scores[:own_users] + scores[own_users:]
            if first_time:
                strengths = mask * ((1.0 + CONFIDENCE) - CONFIDENCE * scores)
            else:
                strengths = mask * scores
            s_high = strengths.astype(BF16)
            s_low = (strengths - s_high.astype(F32)).astype(BF16)
            both = lax.dot_general(
                jnp.concatenate([s_high, s_low], axis=0), item, (((1,), (1,)), ((), ())),
                preferred_element_type=F32,
            )
            running = both[:own_users] + both[own_users:] + table_smem[3, s].astype(F32) * running
            terms[s] = running
            return running

        lax.fori_loop(0, tile_total, step, jnp.zeros((own_users, 128), F32), unroll=UNROLL)
        return jnp.concatenate([jnp.where(table_smem[6, b] > 0, terms[table_smem[5, b]], 0.0) for b in range(blocks)], axis=0)

    def dense_part(vectors):
        return (
            jnp.dot(vectors, gram[...].reshape(128, 128), precision=HIGHEST, preferred_element_type=F32)
            + RIDGE * vectors
        )

    def sums_copy(at, peer, j, slot):
        return remote(sums_send.at[at], sums_recv.at[at, slot], s_send.at[at, j], s_recv.at[at, slot], peer(j))

    def all_sums(products, meanwhile):
        rows = [jnp.sum(p, axis=0, keepdims=True) for p in products]
        rows.append(jnp.zeros((8 - len(rows), 128), F32))
        total = jnp.sum(jnp.concatenate(rows, axis=0), axis=1, keepdims=True)
        at_lane = lax.broadcasted_iota(jnp.int32, (8, 128), 0) == lax.broadcasted_iota(jnp.int32, (8, 128), 1)
        total = jnp.sum(jnp.where(at_lane, total, 0.0), axis=0, keepdims=True)
        for at, (peer, own) in enumerate(((peer_a, own_a), (peer_b, own_b))):
            sums_send[at] = total
            others(own, GROUP, lambda j: sums_copy(at, peer, j, own).start())
            sums_recv[at, own] = total
            meanwhile[at]()
            others(own, GROUP, lambda j: sums_copy(at, peer, j, j).wait_recv())
            total = jnp.sum(sums_recv[at], axis=0)
        return [total[:, i : i + 1] for i in range(len(products))]

    def out_copy(index, j, slot):
        return remote(
            out_send.at[index, j], out_recv.at[index, slot], o_send.at[index, j], o_recv.at[index, slot], peer_c(j)
        )

    def out_begin(index, vectors):
        out_send[index] = vectors.T.reshape(n_cols, col_width, blocks * own_users)
        others(col, n_cols, lambda j: out_copy(index, j, col).start())
        out_recv[index, col] = out_send[index, col]

    def out_end(index):
        others(col, n_cols, lambda j: out_copy(index, j, j).wait_recv())

    z_step(0, 0)
    mask_copy.start()
    others(own_p, PLANE, lambda j: ask_copy(j, own_p).start())
    asked[own_p] = ask[...]
    others(col, n_cols, lambda j: item_copy(j, col).start())
    z_step(0, 1)
    others(col, n_cols, lambda j: user_copy(j, col).start())
    items_recv[own_cols, :] = item_quarter_ref(col)[...]
    users_recv[own_cols, :] = users_send[col]

    def asked_ready():
        others(own_p, PLANE, lambda j: ask_copy(j, j).wait_recv())
        asked_rows[...] = asked[:, 0, :]
        to_smem = pltpu.make_async_copy(asked_rows, asked_smem, smem_sem)
        to_smem.start()
        to_smem.wait()
        pltpu.make_async_copy(table, table_smem, table_sem).wait()

    span = last_step + 2
    def first_half():
        others(col, n_cols, lambda j: user_copy(j, j).wait_recv())
        state_x[...] = users_recv[...].T
        mask_copy.wait()
        x_end(1)
        state_r[...] = sparse_part(state_x[...], (0,), True)

    def gram_middle():
        x_end(0)
        gram_2()

    events = []
    for piece, start in enumerate(STARTS):
        for step in range(span):
            if (piece, step) not in ((0, 0), (0, 1)):
                events.append((start + step, functools.partial(z_step, piece, step)))
            if step == span - 2:
                if piece == 0:
                    events.append((start + step, asked_ready))
                events.append((start + step, functools.partial(plane_begin, piece, 0)))
            if step == span - 1:
                events.append((start + step, functools.partial(plane_begin, piece, 1)))
        events.append((start + span + PACK_AFTER, functools.partial(x_begin, piece)))
        events.append((start + span + PASS_AFTER, functools.partial(x_forward, piece)))
    events.append((STARTS[0] + span, gram_1))
    events.append((STARTS[0] + span + 2, gram_middle))
    events.append((STARTS[0] + span + 4, gram_3))
    events.append((STARTS[-1] + span, first_half))
    for _, event in sorted(events, key=lambda item: item[0]):
        event()
    others(own_a, GROUP, lambda j: gram_third(j, j).wait_recv())
    state_r[...] -= dense_part(state_x[...])
    x_end(2)
    x_end(3)

    state_r[...] += sparse_part(state_x[...], (1,), True)
    out_begin(0, state_r[...])
    image[...] = dense_part(state_r[...]) + CONFIDENCE * sparse_part(state_r[...], (0, 1), False)

    full = gram[...].reshape(128, 128)
    diagonal = lax.broadcasted_iota(jnp.int32, full.shape, 0) == lax.broadcasted_iota(jnp.int32, full.shape, 1)
    trace = jnp.sum(jnp.sum(jnp.where(diagonal, full, 0.0), axis=0, keepdims=True), axis=1, keepdims=True)
    theta = 1.0 / (trace * (1.0 / 128) + RIDGE)
    state_d[...] = state_r[...] - theta * image[...]
    image_w = dense_part(state_d[...]) + CONFIDENCE * sparse_part(state_d[...], (0, 1), False)

    def images_out():
        out_begin(2, image_w)
        out_begin(1, image[...])

    def fetch_sent():
        others(own_p, PLANE, lambda j: ask_copy(j, own_p).wait_send())
        others(col, n_cols, lambda j: item_copy(j, col).wait_send())
        others(col, n_cols, lambda j: user_copy(j, col).wait_send())
        others(own_a, GROUP, lambda j: gram_first(j, own_a).wait_send())
        others(own_b, GROUP, lambda j: gram_second(j, own_b).wait_send())
        others(own_a, GROUP, lambda j: gram_third(j, own_a).wait_send())
        for piece in range(PIECES):
            for step in range(last_step + 1):
                for way in range(2):
                    for h in range(CHUNKS):
                        if z_travels(step, way, h):
                            z_copy(piece, way, step, h).wait_send()
            for half in range(2):
                others(own_p, PLANE, lambda j: plane_copy(piece, half, j, own_p).wait_send())
            for kind, owner, peer in ((0, col, right), (1, col, right), (2, col, left), (3, col, left), (4, left, right), (5, right, left)):
                x_copy(piece, kind, owner, peer).wait_send()

    rr, rw, ww, ri, wi, rj, wj = all_sums(
        [
            state_r[...] * state_r[...],
            state_r[...] * state_d[...],
            state_d[...] * state_d[...],
            state_r[...] * image[...],
            state_d[...] * image[...],
            state_r[...] * image_w,
            state_d[...] * image_w,
        ],
        (images_out, fetch_sent),
    )
    delta = rw / (rr - rw)
    more = 1.0 + delta
    alpha_0 = theta * more
    norm_1 = delta * delta * rr - 2.0 * delta * more * rw + more * more * ww
    beta = norm_1 / rr
    curve_1 = (
        more * more * wj
        - delta * more * (wi + rj)
        + delta * delta * ri
        + beta * (more * (wi + rj) - 2.0 * delta * ri)
        + beta * beta * ri
    )
    alpha_1 = norm_1 / curve_1

    for index in range(3):
        out_end(index)
    for block in range(blocks):
        lanes = pl.ds((block // 2) * 128, 128)
        for side in range(n_cols // 2):
            start_r, image_r, image_d = [
                interleave(out_recv[i, 2 * side, :, lanes], out_recv[i, 2 * side + 1, :, lanes], block % 2 == 1)
                for i in range(3)
            ]
            here = pl.ds(block * 256 + side * 128, 128)
            mid_r = more * (start_r - theta * image_r) - delta * start_r
            mid_x = users_ref[:, here] + alpha_0 * start_r
            solution_ref[:, here] = mid_x + alpha_1 * (mid_r + beta * start_r)
            residual_ref[:, here] = mid_r - alpha_1 * (more * image_d + (beta - delta) * image_r)

    others(own_a, GROUP, lambda j: sums_copy(0, peer_a, j, own_a).wait_send())
    others(own_b, GROUP, lambda j: sums_copy(1, peer_b, j, own_b).wait_send())
    for index in range(3):
        others(col, n_cols, lambda j: out_copy(index, j, col).wait_send())


def on_device(user_factors, item_factors, tile_user, tile_item, tile_count, tile_mask):
    n_cols = lax.axis_size("cols")
    col_width, users = user_factors.shape
    slots, tile_rows, tile_cols = tile_mask.shape
    width = col_width * n_cols
    blocks = users // tile_rows
    item_blocks = item_factors.shape[1] // tile_rows
    own_users = tile_rows // n_cols
    mine = blocks * own_users
    item_quarter = item_factors.shape[1] // n_cols
    vmem = pl.BlockSpec(memory_space=pltpu.VMEM)
    hbm = pl.BlockSpec(memory_space=pl.ANY)
    piece = width // GROUP
    dma = pltpu.SemaphoreType.DMA
    out = jax.ShapeDtypeStruct((col_width, users), F32)
    return pl.pallas_call(
        kernel,
        out_shape=(out, out),
        in_specs=[hbm] * 6,
        out_specs=(vmem, vmem),
        scratch_shapes=[
            pltpu.SMEM(tile_count.shape, jnp.int32),
            pltpu.SMEM(tile_user.shape, jnp.int32),
            pltpu.SMEM(tile_item.shape, jnp.int32),
            pltpu.VMEM((col_width, users), F32),
            pltpu.VMEM((col_width, item_factors.shape[1]), BF16),
            pltpu.VMEM((128, 128), jnp.int32),
            pltpu.VMEM((128, 128), jnp.int32),
            pltpu.VMEM((8, 128), jnp.int32),
            pltpu.SMEM((8, 128), jnp.int32),
            pltpu.VMEM((1, 128), jnp.int32),
            pltpu.VMEM((PLANE, 1, 128), jnp.int32),
            pltpu.VMEM((PLANE, 128), jnp.int32),
            pltpu.SMEM((PLANE, 128), jnp.int32),
            *[pltpu.VMEM((Z_CHIPS - 1, item_blocks, 16, 128), BF16)] * PIECES,
            *[pltpu.VMEM((item_blocks, 16, 128), BF16)] * PIECES,
            pltpu.VMEM((PIECES, PLANE, SLOTS, 16, 128), BF16),
            *[pltpu.VMEM((PLANE, SLOTS, 16, 128), BF16)] * PIECES,
            pltpu.VMEM((2, slots, width, 128), BF16),
            pltpu.VMEM((slots, own_users, tile_cols), BF16),
            pltpu.VMEM((n_cols, col_width, mine), F32),
            pltpu.VMEM((width, mine), F32),
            pltpu.VMEM((width, item_quarter), BF16),
            pltpu.VMEM((GROUP, piece, width), F32),
            pltpu.VMEM((GROUP, piece, width), F32),
            pltpu.VMEM((piece, width), F32),
            pltpu.VMEM((GROUP, piece, width), F32),
            pltpu.VMEM((GROUP, piece, width), F32),
            pltpu.VMEM((2, 1, 128), F32),
            pltpu.VMEM((2, GROUP, 1, 128), F32),
            pltpu.VMEM((blocks, 2 * own_users, width), BF16),
            pltpu.VMEM((slots, own_users, width), F32),
            pltpu.VMEM((mine, width), F32),
            pltpu.VMEM((mine, width), F32),
            pltpu.VMEM((mine, width), F32),
            pltpu.VMEM((mine, width), F32),
            pltpu.VMEM((3, n_cols, col_width, mine), F32),
            pltpu.VMEM((3, n_cols, col_width, mine), F32),
            dma((3,)),
            dma,
            dma,
            dma,
            dma,
            dma,
            dma((PLANE,)),
            dma((PLANE,)),
            dma((PIECES, 2, Z_CHIPS // 2, CHUNKS)),
            dma((PIECES, 2, Z_CHIPS // 2, CHUNKS)),
            dma((PIECES, 2, PLANE)),
            dma((PIECES, 2, PLANE)),
            dma((PIECES, 6)),
            dma((PIECES, 6)),
            dma((n_cols,)),
            dma((n_cols,)),
            dma((n_cols,)),
            dma((n_cols,)),
            dma((3, GROUP)),
            dma((3, GROUP)),
            dma((2, GROUP)),
            dma((2, GROUP)),
            dma((3, n_cols)),
            dma((3, n_cols)),
        ],
        compiler_params=pltpu.CompilerParams(
            collective_id=0, has_side_effects=True, vmem_limit_bytes=VMEM_BYTES
        ),
    )(tile_count, tile_user, tile_item, user_factors, item_factors, tile_mask)


def solution(mesh):
    return jax.shard_map(
        on_device,
        mesh=mesh,
        in_specs=(
            P("cols", "rows"),
            P("cols", "rows"),
            P("rows"),
            P("rows"),
            P("rows"),
            P("rows", None, None),
        ),
        out_specs=(P("cols", "rows"), P("cols", "rows")),
        check_vma=False,
    )
```
